32 devices in a mesh: pipe: 4 (over z), expert: 8 (over y, x, core).
Axes of the slice: x: 2, y: 2, z: 4, core: 2. Of those that a mesh axis runs over, the one named last changes fastest.
Arguments:
- inputs: bfloat16 [4, 1024, 4096], P('pipe', 'expert'), may hold values from -6 to 6
- upstream: bfloat16 [4, 1024, 4096], P('pipe', 'expert'), may hold values from -24 to 24
- route: int32 [4, 1024, 8], P('pipe', 'expert'), may hold values from 0 to 127, as said below
- prob: float32 [4, 1024, 8], P('pipe', 'expert'), may hold values from 0.05 to 0.4
- gate_up: bfloat16 [4, 8, 4096, 384], P('pipe', 'expert'), may hold values from -0.09375 to 0.09375
- down: bfloat16 [4, 8, 192, 4096], P('pipe', 'expert'), may hold values from -0.15625 to 0.15625
Outputs:
- grad_input: bfloat16 [4, 1024, 4096], P('pipe', 'expert')
- grad_gate_up: bfloat16 [4, 8, 4096, 384], P('pipe', 'expert')
- grad_down: bfloat16 [4, 8, 192, 4096], P('pipe', 'expert')
The draws below stay inside these ranges and needn't reach their ends.
Inputs may be any that keep to these rules, and one draw needn't show every extreme that they name: `route`: each token names 8 different experts and at most one expert below 1. In each aligned block of 128 tokens of a section every expert below 1 is named by 1 to 8 tokens; one such expert, the same for all blocks, is named by exactly 8 tokens of every block.
All inputs are finite; a program needn't handle non-finite values.
Results may differ from the reference program's by a relative error of at most 0.014.
Values may be sent and summed in bfloat16 or wider, within the bound.
A program may use at most 128 MiB of HBM per device.

```python
import math
import jax
import jax.numpy as jnp
from jax import lax

D = 4096
H = 1536
EXPERTS = 128
TOPK = 8
SPLIT = 8
CAP = 8
TOK_DEV = 128
HS = 192
EXP_FLIGHT = 1
TOKENS = 1024
N_PIPE = 4
N_EXPERT = 8


def draw_route(key, part):
    keys = jax.random.split(key, 5)
    blocks = N_PIPE * (TOKENS // TOK_DEV)
    flight = EXP_FLIGHT
    hot_one = jax.random.randint(keys[0], (), 0, flight)
    counts = jax.random.randint(keys[1], (blocks, flight), 1, CAP + 1)
    counts = jnp.where(jnp.arange(flight)[None, :] == hot_one, CAP, counts)
    ends = jnp.cumsum(counts, axis=1)
    scores = jax.random.randint(keys[2], (blocks, TOK_DEV), 0, 2 ** 20) * TOK_DEV + jnp.arange(TOK_DEV)[None, :]
    rank = jnp.argsort(jnp.argsort(scores, axis=1, stable=True), axis=1, stable=True).astype(jnp.int32)
    has_one = rank < ends[:, -1:]
    chosen = jnp.sum((rank[:, :, None] >= ends[:, None, :]).astype(jnp.int32), axis=2)
    others_n = EXPERTS - flight
    other_scores = jax.random.randint(keys[3], (blocks, TOK_DEV, others_n), 0, 2 ** 16) * others_n + jnp.arange(others_n)[None, None, :]
    picked = lax.top_k(other_scores, TOPK)[1].astype(jnp.int32) + flight
    where_slot = jax.random.randint(keys[4], (blocks, TOK_DEV), 0, TOPK)
    place = has_one[:, :, None] & (jnp.arange(TOPK)[None, None, :] == where_slot[:, :, None])
    ids = jnp.where(place, chosen[:, :, None], picked)
    return ids.reshape(N_PIPE, TOKENS, TOPK).astype(jnp.int32)


def shard_levels(own_key, extent, cuts, low, top_value):
    gain = 1.0
    for position, parts in cuts:
        steps = jax.random.uniform(jax.random.fold_in(jax.random.fold_in(own_key, 6), position), (parts,), jnp.float32, low / len(cuts), top_value / len(cuts))
        gain = gain * jnp.repeat(jnp.exp(steps), extent[position] // parts).reshape((-1,) + (1,) * (len(extent) - 1 - position))
    return gain


def gaussian(own_key, shape, scale, limit, pieces=(), held_as=jnp.bfloat16):
    entries = jax.random.normal(own_key, shape, jnp.float32) * scale
    if len(pieces) > 0:
        entries = shard_levels(own_key, shape, pieces, -0.22, 0.18) * entries
    return jnp.clip(entries, min=-limit, max=limit).astype(held_as)


def setup_inputs(seed: int = 0) -> dict:
    key_of = jax.random.split(jax.random.key(seed), 7)
    return {
        "inputs": gaussian(key_of[0], (N_PIPE, TOKENS, D), 1.0, 6.0, ((0, 4), (1, 8))),
        "upstream": gaussian(key_of[1], (N_PIPE, TOKENS, D), 4.0, 24.0, ((0, 4), (1, 8))),
        "route": draw_route(jax.random.fold_in(key_of[6], 71), 0),
        "prob": jnp.clip(jnp.exp(math.log(0.4) - 2.0794415 * jax.random.uniform(key_of[3], (N_PIPE, TOKENS, TOPK), jnp.float32) ** shard_levels(key_of[3], (N_PIPE, TOKENS, TOPK), ((0, 4), (1, 8)), -0.2, 0.2)), 0.05, 0.4),
        "gate_up": gaussian(key_of[4], (N_PIPE, N_EXPERT, D, 2 * HS), D ** -0.5, 0.09375, ((0, 4), (1, 8))),
        "down": gaussian(key_of[5], (N_PIPE, N_EXPERT, HS, D), H ** -0.5, 0.15625, ((0, 4), (1, 8))),
    }


def reference(inputs, upstream, route, prob, gate_up, down):
    tokens = inputs.shape[1]
    width = inputs.shape[2]
    blocks = tokens // TOK_DEV
    hidden_cols = down.shape[2]
    slot_ids = jnp.arange(CAP, dtype=jnp.int32)
    grad_inputs = []
    grad_gu_all = []
    grad_down_all = []
    for section in range(N_PIPE):
        arrived = upstream[(section + 1) % N_PIPE].astype(jnp.float32)
        layer_in = inputs[section]
        total = jnp.zeros((tokens, width), jnp.float32)
        gu_rows = []
        dn_rows = []
        for expert in range(EXP_FLIGHT):
            hits = route[section] == expert
            member = jnp.any(hits, axis=1).astype(jnp.int32)
            weight = jnp.sum(jnp.where(hits, prob[section], jnp.float32(0.0)), axis=1)
            member_b = member.reshape(blocks, TOK_DEV)
            rank = jnp.cumsum(member_b, axis=1) - member_b
            select = (member_b[:, None, :] == 1) & (rank[:, None, :] == slot_ids[None, :, None])
            picker = select.astype(jnp.float32)
            x_blocks = layer_in.reshape(blocks, TOK_DEV, width).astype(jnp.float32)
            rows_x = jnp.einsum("bct,btd->bcd", picker, x_blocks, precision=lax.Precision.HIGHEST).reshape(-1, width).astype(jnp.bfloat16)
            scaled = (arrived * weight[:, None]).reshape(blocks, TOK_DEV, width)
            rows_e = jnp.einsum("bct,btd->bcd", picker, scaled, precision=lax.Precision.HIGHEST).reshape(-1, width).astype(jnp.bfloat16)
            part_total = jnp.zeros((blocks * CAP, width), jnp.float32)
            for slice_idx in range(SPLIT):
                row = expert * SPLIT + slice_idx
                w_both = gate_up[section, row]
                w_down = down[section, row]
                both = jnp.dot(rows_x, w_both, preferred_element_type=jnp.float32)
                pre_gate = both[:, :hidden_cols]
                pre_up = both[:, hidden_cols:]
                sigma = jax.nn.sigmoid(pre_gate)
                silu_val = pre_gate * sigma
                hidden = (silu_val * pre_up).astype(jnp.bfloat16)
                grad_hidden = jnp.dot(rows_e, w_down.T, preferred_element_type=jnp.float32)
                grad_a = (grad_hidden * pre_up * sigma * (1.0 + pre_gate * (1.0 - sigma))).astype(jnp.bfloat16)
                grad_u = (grad_hidden * silu_val).astype(jnp.bfloat16)
                grad_both = jnp.concatenate([grad_a, grad_u], axis=1)
                dn_rows.append(jnp.dot(hidden.T, rows_e, preferred_element_type=jnp.float32).astype(jnp.bfloat16))
                gu_rows.append(jnp.dot(rows_x.T, grad_both, preferred_element_type=jnp.float32).astype(jnp.bfloat16))
                part = jnp.dot(grad_both, w_both.T, preferred_element_type=jnp.float32).astype(jnp.bfloat16)
                part_total = part_total + part.astype(jnp.float32)
            back = jnp.einsum("bct,bcd->btd", picker, part_total.reshape(blocks, CAP, width), precision=lax.Precision.HIGHEST)
            total = total + back.reshape(tokens, width)
        grad_inputs.append(total.astype(jnp.bfloat16))
        grad_gu_all.append(jnp.stack(gu_rows))
        grad_down_all.append(jnp.stack(dn_rows))
    return jnp.stack(grad_inputs), jnp.stack(grad_gu_all), jnp.stack(grad_down_all)
```

```python
import functools

import jax
import jax.numpy as jnp
from jax import lax
from jax.experimental import pallas as pl
from jax.experimental.pallas import tpu as pltpu
from jax.sharding import PartitionSpec as P

SPLIT = 8
CAP = 8
CORES = 2
E_PARTS = 2
OUT_PARTS = 4
MESH = pl.DeviceIdType.MESH
F32 = jnp.float32
BF16 = jnp.bfloat16


def dot(a, b, dims):
    return lax.dot_general(a, b, (dims, ((), ())), preferred_element_type=F32)


def remote(src, dst, send, recv, target):
    return pltpu.make_async_remote_copy(
        src_ref=src, dst_ref=dst, send_sem=send, recv_sem=recv, device_id=target, device_id_type=MESH
    )


def exchange(
    sections, chips, flight,
    x_hbm, u_hbm, route_hbm, prob_hbm, gu_hbm, dn_hbm,
    ggu, gdn, sums, sel_out,
    x_v, u_v, route_v, prob_v, w_gu, w_dn,
    s_out, s_in, xb, xg, eb, er, eg, pair_in, keep, ro, rin,
    local, s_sem, x_send, x_recv, xf_send, xf_recv,
    z_send, z_recv, e_send, e_recv, ef_send, ef_recv,
    p_send, p_recv, r_send, r_recv,
):
    section = lax.axis_index("pipe")
    me = lax.axis_index("expert")
    chip, core = me // CORES, me % CORES
    mine = me // SPLIT
    sibling = {"expert": me + 1 - 2 * core}
    ahead = {"pipe": (section + 1) % sections}
    behind = {"pipe": (section + sections - 1) % sections}
    width = x_v.shape[1]
    tokens = x_v.shape[0]
    hid = w_dn.shape[0]

    def chip_at(d):
        return (chip + d) % chips

    def chip_from(d):
        return (chip + chips - d) % chips

    def peer(d):
        return {"expert": chip_at(d) * CORES + core}

    loads = [
        pltpu.make_async_copy(src, dst, local.at[k])
        for k, (src, dst) in enumerate(
            (
                (route_hbm.at[0], route_v),
                (prob_hbm.at[0], prob_v),
                (x_hbm.at[0], x_v),
                (u_hbm.at[0], u_v),
                (gu_hbm.at[0, 0], w_gu),
                (dn_hbm.at[0, 0], w_dn),
            )
        )
    ]
    for load in loads:
        load.start()
    barrier = pltpu.get_barrier_semaphore()
    for target in [sibling, ahead, behind] + [peer(d) for d in range(1, chips)]:
        pl.semaphore_signal(barrier, inc=1, device_id=target, device_id_type=MESH)
    loads[0].wait()
    loads[1].wait()
    before = (
        lax.broadcasted_iota(jnp.int32, (tokens, tokens), 0)
        < lax.broadcasted_iota(jnp.int32, (tokens, tokens), 1)
    ).astype(F32).astype(BF16)
    slots = lax.broadcasted_iota(jnp.int32, (CAP, tokens), 0).astype(F32)
    picks = []
    for e in range(flight):
        hit = route_v[...] == e
        member = jnp.max(jnp.where(hit, 1.0, 0.0), axis=0, keepdims=True)
        weight = jnp.sum(jnp.where(hit, prob_v[...], 0.0), axis=0, keepdims=True)
        member = jnp.broadcast_to(member, (CAP, tokens))
        rank = dot(member.astype(BF16), before, ((1,), (0,)))
        chosen = jnp.where((member > 0.0) & (rank == slots), 1.0, 0.0)
        sel_out[e] = chosen
        s_out[e] = chosen * weight
        picks.append(chosen.astype(BF16))
    pl.semaphore_wait(barrier, chips + 2)

    send_s = remote(s_out, s_in, s_sem.at[0], s_sem.at[1], ahead)
    send_s.start()
    sends = [send_s]

    loads[2].wait()
    for e in range(flight):
        xb[e] = dot(picks[e], x_v[...], ((1,), (0,))).astype(BF16)
    for d in range(1, chips):
        copy = remote(
            xb.at[chip_at(d) * CORES // SPLIT], xg.at[core, chip], x_send.at[d], x_recv.at[d], peer(d)
        )
        copy.start()
        sends.append(copy)
    copy = remote(xb.at[mine], xg.at[core, chip], xf_send.at[0], xf_recv.at[0], sibling)
    copy.start()
    sends.append(copy)
    xg[core, chip] = xb[mine]

    loads[3].wait()
    send_s.wait_recv()
    e_cols = width // E_PARTS
    scales, gpicks = [], []
    for e in range(flight):
        weights = s_in[e]
        scales.append(jnp.sum(weights, axis=1, keepdims=True))
        gpicks.append(jnp.where(weights > 0.0, 1.0, 0.0).astype(BF16))
    z_copies = []
    for k in range(E_PARTS):
        cols = pl.ds(k * e_cols, e_cols)
        for e in range(flight):
            eb[e, :, cols] = (dot(gpicks[e], u_v[:, cols], ((1,), (0,))) * scales[e]).astype(BF16)
        copy = remote(eb.at[:, :, cols], er.at[:, :, cols], z_send.at[k], z_recv.at[k], behind)
        copy.start()
        z_copies.append(copy)
    sends.extend(z_copies)

    def relay(buf, d, cols, recv, f_send, f_recv):
        slot = buf.at[core, chip_from(d), :, cols]
        remote(slot, slot, f_send, recv, sibling).wait_recv()
        copy = remote(slot, slot, f_send, f_recv, sibling)
        copy.start()
        sends.append(copy)

    def from_sibling(buf, d, cols, f_send, f_recv):
        slot = buf.at[1 - core, chip_from(d), :, cols]
        remote(slot, slot, f_send, f_recv, sibling).wait_recv()

    every = pl.ds(0, width)
    for d in range(1, chips):
        relay(xg, d, every, x_recv.at[d], xf_send.at[d], xf_recv.at[d])
    for k in range(E_PARTS):
        cols = pl.ds(k * e_cols, e_cols)
        z_copies[k].wait_recv()
        for d in range(1, chips):
            copy = remote(
                er.at[chip_at(d) * CORES // SPLIT, :, cols],
                eg.at[core, chip, :, cols],
                e_send.at[k, d],
                e_recv.at[k, d],
                peer(d),
            )
            copy.start()
            sends.append(copy)
        copy = remote(
            er.at[mine, :, cols], eg.at[core, chip, :, cols], ef_send.at[k, 0], ef_recv.at[k, 0], sibling
        )
        copy.start()
        sends.append(copy)
        eg[core, chip, :, cols] = er[mine, :, cols]
    for d in range(chips):
        from_sibling(xg, d, every, xf_send.at[d], xf_recv.at[d])
    rows = CORES * chips * CAP
    loads[4].wait()
    both = dot(xg[...].reshape(rows, width), w_gu[...], ((1,), (0,)))
    pre_gate = both[:, :hid]
    pre_up = both[:, hid:]
    sigma = jax.nn.sigmoid(pre_gate)
    silu_val = pre_gate * sigma
    hidden = (silu_val * pre_up).astype(BF16)
    slope = pre_up * sigma * (1.0 + pre_gate * (1.0 - sigma))

    loads[5].wait()
    grad_hidden = None
    for k in range(E_PARTS):
        cols = pl.ds(k * e_cols, e_cols)
        for d in range(1, chips):
            relay(eg, d, cols, e_recv.at[k, d], ef_send.at[k, d], ef_recv.at[k, d])
    for k in range(E_PARTS):
        cols = pl.ds(k * e_cols, e_cols)
        for d in range(chips):
            from_sibling(eg, d, cols, ef_send.at[k, d], ef_recv.at[k, d])
        term = dot(eg[:, :, :, cols].reshape(rows, e_cols), w_dn[:, cols], ((1,), (1,)))
        grad_hidden = term if grad_hidden is None else grad_hidden + term
    grad_both = jnp.concatenate([grad_hidden * slope, grad_hidden * silu_val], axis=1).astype(BF16)

    o_cols = width // OUT_PARTS
    pair = []
    for k in range(OUT_PARTS):
        cols = pl.ds(k * o_cols, o_cols)
        part = dot(grad_both, w_gu[cols, :], ((1,), (1,))).astype(BF16)
        keep[:, :, :, cols] = part.reshape(CORES, chips, CAP, o_cols)
        copy = remote(
            keep.at[1 - core, :, :, cols], pair_in.at[:, :, cols], p_send.at[k], p_recv.at[k], sibling
        )
        copy.start()
        pair.append(copy)
    sends.extend(pair)
    for k in range(OUT_PARTS):
        cols = pl.ds(k * o_cols, o_cols)
        pair[k].wait_recv()
        ro[:, :, cols] = (keep[core, :, :, cols].astype(F32) + pair_in[:, :, cols].astype(F32)).astype(BF16)
        for d in range(1, chips):
            copy = remote(
                ro.at[chip_at(d), :, cols], rin.at[chip, :, cols], r_send.at[k, d], r_recv.at[k, d], peer(d)
            )
            copy.start()
            sends.append(copy)
        rin[chip, :, cols] = ro[chip, :, cols]

    for k in range(OUT_PARTS):
        cols = pl.ds(k * o_cols, o_cols)
        x_part = xg[:, :, :, cols].reshape(rows, o_cols)
        ggu[cols, :] = dot(x_part, grad_both, ((0,), (0,))).astype(BF16)
        e_part = eg[:, :, :, cols].reshape(rows, o_cols)
        gdn[:, cols] = dot(hidden, e_part, ((0,), (0,))).astype(BF16)

    per = chips // flight
    for k in range(OUT_PARTS):
        cols = pl.ds(k * o_cols, o_cols)
        for d in range(1, chips):
            slot = rin.at[chip_from(d), :, cols]
            remote(slot, slot, r_send.at[k, d], r_recv.at[k, d], peer(d)).wait_recv()
        for e in range(flight):
            total = rin[e * per, :, cols].astype(F32)
            for q in range(1, per):
                total = total + rin[e * per + q, :, cols].astype(F32)
            sums[e, :, cols] = total.astype(BF16)
    for copy in sends:
        copy.wait_send()


def finish(flight, ggu, gdn, sums, sel, gi_hbm, gu_hbm, dn_hbm, gi_v, sems):
    copies = [
        pltpu.make_async_copy(ggu, gu_hbm.at[0, 0], sems.at[0]),
        pltpu.make_async_copy(gdn, dn_hbm.at[0, 0], sems.at[1]),
    ]
    for copy in copies:
        copy.start()
    total = None
    for e in range(flight):
        term = dot(sel[e].astype(BF16), sums[e], ((0,), (0,)))
        total = term if total is None else total + term
    gi_v[...] = total.astype(BF16)
    last = pltpu.make_async_copy(gi_v, gi_hbm.at[0], sems.at[2])
    last.start()
    for copy in copies + [last]:
        copy.wait()


def shards(inputs, upstream, route, prob, gate_up, down):
    sections = lax.axis_size("pipe")
    groups = lax.axis_size("expert")
    chips = groups // CORES
    flight = groups // SPLIT
    _, tokens, width = inputs.shape
    slots = route.shape[2]
    both_cols = gate_up.shape[3]
    hid = down.shape[2]
    dma = pltpu.SemaphoreType.DMA
    anywhere = pl.BlockSpec(memory_space=pl.ANY)
    vmem = pl.BlockSpec(memory_space=pltpu.VMEM)
    kept = pltpu.VMEM
    ggu, gdn, sums, sel = pl.pallas_call(
        functools.partial(exchange, sections, chips, flight),
        out_shape=(
            kept((width, both_cols), BF16),
            kept((hid, width), BF16),
            kept((flight, CAP, width), BF16),
            kept((flight, CAP, tokens), F32),
        ),
        in_specs=[anywhere] * 6,
        out_specs=(vmem,) * 4,
        scratch_shapes=[
            pltpu.VMEM((tokens, width), BF16),
            pltpu.VMEM((tokens, width), BF16),
            pltpu.VMEM((slots, tokens), jnp.int32),
            pltpu.VMEM((slots, tokens), F32),
            pltpu.VMEM((width, both_cols), BF16),
            pltpu.VMEM((hid, width), BF16),
            pltpu.VMEM((flight, CAP, tokens), F32),
            pltpu.VMEM((flight, CAP, tokens), F32),
            pltpu.VMEM((flight, CAP, width), BF16),
            pltpu.VMEM((CORES, chips, CAP, width), BF16),
            pltpu.VMEM((flight, CAP, width), BF16),
            pltpu.VMEM((flight, CAP, width), BF16),
            pltpu.VMEM((CORES, chips, CAP, width), BF16),
            pltpu.VMEM((chips, CAP, width), BF16),
            pltpu.VMEM((CORES, chips, CAP, width), BF16),
            pltpu.VMEM((chips, CAP, width), BF16),
            pltpu.VMEM((chips, CAP, width), BF16),
            dma((6,)),
            dma((2,)),
            dma((chips,)),
            dma((chips,)),
            dma((chips,)),
            dma((chips,)),
            dma((E_PARTS,)),
            dma((E_PARTS,)),
            dma((E_PARTS, chips)),
            dma((E_PARTS, chips)),
            dma((E_PARTS, chips)),
            dma((E_PARTS, chips)),
            dma((OUT_PARTS,)),
            dma((OUT_PARTS,)),
            dma((OUT_PARTS, chips)),
            dma((OUT_PARTS, chips)),
        ],
        compiler_params=pltpu.CompilerParams(
            collective_id=0, has_side_effects=True, vmem_limit_bytes=40 * 2**20
        ),
    )(inputs, upstream, jnp.swapaxes(route, 1, 2), jnp.swapaxes(prob, 1, 2), gate_up, down)
    return pl.pallas_call(
        functools.partial(finish, flight),
        out_shape=(
            jax.ShapeDtypeStruct(inputs.shape, BF16),
            jax.ShapeDtypeStruct(gate_up.shape, BF16),
            jax.ShapeDtypeStruct(down.shape, BF16),
        ),
        in_specs=[vmem] * 4,
        out_specs=(anywhere,) * 3,
        scratch_shapes=[pltpu.VMEM((tokens, width), BF16), dma((3,))],
        compiler_params=pltpu.CompilerParams(vmem_limit_bytes=16 * 2**20),
    )(ggu, gdn, sums, sel)


def solution(mesh):
    placed = (
        P("pipe", "expert", None),
        P("pipe", "expert", None),
        P("pipe", "expert", None),
        P("pipe", "expert", None),
        P("pipe", "expert", None, None),
        P("pipe", "expert", None, None),
    )
    return jax.shard_map(
        shards,
        mesh=mesh,
        in_specs=placed,
        out_specs=(
            P("pipe", "expert", None),
            P("pipe", "expert", None, None),
            P("pipe", "expert", None, None),
        ),
        check_vma=False,
    )
```

```python
import functools

import jax
import jax.numpy as jnp
from jax import lax
from jax.experimental import pallas as pl
from jax.experimental.pallas import tpu as pltpu
from jax.sharding import PartitionSpec as P

SPLIT = 8
CAP = 8
CORES = 2
E_PARTS = 2
OUT_PARTS = 4
MESH = pl.DeviceIdType.MESH
F32 = jnp.float32
BF16 = jnp.bfloat16


def dot(a, b, dims):
    return lax.dot_general(a, b, (dims, ((), ())), preferred_element_type=F32)


def remote(src, dst, send, recv, target):
    return pltpu.make_async_remote_copy(
        src_ref=src, dst_ref=dst, send_sem=send, recv_sem=recv, device_id=target, device_id_type=MESH
    )


def exchange(
    sections, chips, flight,
    x_hbm, u_hbm, route_hbm, prob_hbm, gu_hbm, dn_hbm,
    ggu, gdn, sums, sel_out,
    x_v, u_v, route_v, prob_v, w_gu, w_dn,
    s_out, s_in, xb, xg, eb, er, eg, pair_in, keep, ro, rin,
    local, s_sem, x_send, x_recv, xf_send, xf_recv,
    z_send, z_recv, e_send, e_recv, ef_send, ef_recv,
    p_send, p_recv, r_send, r_recv,
):
    section = lax.axis_index("pipe")
    me = lax.axis_index("expert")
    chip, core = me // CORES, me % CORES
    mine = me // SPLIT
    sibling = {"expert": me + 1 - 2 * core}
    ahead = {"pipe": (section + 1) % sections}
    behind = {"pipe": (section + sections - 1) % sections}
    width = x_v.shape[1]
    tokens = x_v.shape[0]
    hid = w_dn.shape[0]

    def chip_at(d):
        return (chip + d) % chips

    def chip_from(d):
        return (chip + chips - d) % chips

    def peer(d):
        return {"expert": chip_at(d) * CORES + core}

    loads = [
        pltpu.make_async_copy(src, dst, local.at[k])
        for k, (src, dst) in enumerate(
            (
                (route_hbm.at[0], route_v),
                (prob_hbm.at[0], prob_v),
                (x_hbm.at[0], x_v),
                (u_hbm.at[0], u_v),
                (gu_hbm.at[0, 0], w_gu),
                (dn_hbm.at[0, 0], w_dn),
            )
        )
    ]
    for load in loads:
        load.start()
    barrier = pltpu.get_barrier_semaphore()
    for target in [sibling, ahead, behind] + [peer(d) for d in range(1, chips)]:
        pl.semaphore_signal(barrier, inc=1, device_id=target, device_id_type=MESH)
    loads[0].wait()
    loads[1].wait()
    before = (
        lax.broadcasted_iota(jnp.int32, (tokens, tokens), 0)
        < lax.broadcasted_iota(jnp.int32, (tokens, tokens), 1)
    ).astype(F32).astype(BF16)
    slots = lax.broadcasted_iota(jnp.int32, (CAP, tokens), 0).astype(F32)
    picks = []
    for e in range(flight):
        hit = route_v[...] == e
        member = jnp.max(jnp.where(hit, 1.0, 0.0), axis=0, keepdims=True)
        weight = jnp.sum(jnp.where(hit, prob_v[...], 0.0), axis=0, keepdims=True)
        member = jnp.broadcast_to(member, (CAP, tokens))
        rank = dot(member.astype(BF16), before, ((1,), (0,)))
        chosen = jnp.where((member > 0.0) & (rank == slots), 1.0, 0.0)
        sel_out[e] = chosen
        s_out[e] = chosen * weight
        picks.append(chosen.astype(BF16))
    pl.semaphore_wait(barrier, chips + 2)

    send_s = remote(s_out, s_in, s_sem.at[0], s_sem.at[1], ahead)
    send_s.start()
    sends = [send_s]

    loads[2].wait()
    for e in range(flight):
        xb[e] = dot(picks[e], x_v[...], ((1,), (0,))).astype(BF16)
    for d in range(1, chips):
        copy = remote(
            xb.at[chip_at(d) * CORES // SPLIT], xg.at[core, chip], x_send.at[d], x_recv.at[d], peer(d)
        )
        copy.start()
        sends.append(copy)
    copy = remote(xb.at[mine], xg.at[core, chip], xf_send.at[0], xf_recv.at[0], sibling)
    copy.start()
    sends.append(copy)
    xg[core, chip] = xb[mine]

    loads[3].wait()
    send_s.wait_recv()
    e_cols = width // E_PARTS
    scales, gpicks = [], []
    for e in range(flight):
        weights = s_in[e]
        scales.append(jnp.sum(weights, axis=1, keepdims=True))
        gpicks.append(jnp.where(weights > 0.0, 1.0, 0.0).astype(BF16))
    z_copies = []
    for k in range(E_PARTS):
        cols = pl.ds(k * e_cols, e_cols)
        for e in range(flight):
            eb[e, :, cols] = (dot(gpicks[e], u_v[:, cols], ((1,), (0,))) * scales[e]).astype(BF16)
        copy = remote(eb.at[:, :, cols], er.at[:, :, cols], z_send.at[k], z_recv.at[k], behind)
        copy.start()
        z_copies.append(copy)
    sends.extend(z_copies)

    def relay(buf, d, cols, recv, f_send, f_recv):
        slot = buf.at[core, chip_from(d), :, cols]
        remote(slot, slot, f_send, recv, sibling).wait_recv()
        copy = remote(slot, slot, f_send, f_recv, sibling)
        copy.start()
        sends.append(copy)

    def from_sibling(buf, d, cols, f_send, f_recv):
        slot = buf.at[1 - core, chip_from(d), :, cols]
        remote(slot, slot, f_send, f_recv, sibling).wait_recv()

    every = pl.ds(0, width)
    for d in range(1, chips):
        relay(xg, d, every, x_recv.at[d], xf_send.at[d], xf_recv.at[d])
    for k in range(E_PARTS):
        cols = pl.ds(k * e_cols, e_cols)
        z_copies[k].wait_recv()
        for d in range(1, chips):
            copy = remote(
                er.at[chip_at(d) * CORES // SPLIT, :, cols],
                eg.at[core, chip, :, cols],
                e_send.at[k, d],
                e_recv.at[k, d],
                peer(d),
            )
            copy.start()
            sends.append(copy)
        copy = remote(
            er.at[mine, :, cols], eg.at[core, chip, :, cols], ef_send.at[k, 0], ef_recv.at[k, 0], sibling
        )
        copy.start()
        sends.append(copy)
        eg[core, chip, :, cols] = er[mine, :, cols]
    for d in range(chips):
        from_sibling(xg, d, every, xf_send.at[d], xf_recv.at[d])
    rows = CORES * chips * CAP
    loads[4].wait()
    both = dot(xg[...].reshape(rows, width), w_gu[...], ((1,), (0,)))
    pre_gate = both[:, :hid]
    pre_up = both[:, hid:]
    sigma = jax.nn.sigmoid(pre_gate)
    silu_val = pre_gate * sigma
    hidden = (silu_val * pre_up).astype(BF16)
    slope = pre_up * sigma * (1.0 + pre_gate * (1.0 - sigma))

    loads[5].wait()
    grad_hidden = None
    for k in range(E_PARTS):
        cols = pl.ds(k * e_cols, e_cols)
        for d in range(1, chips):
            relay(eg, d, cols, e_recv.at[k, d], ef_send.at[k, d], ef_recv.at[k, d])
    for k in range(E_PARTS):
        cols = pl.ds(k * e_cols, e_cols)
        for d in range(chips):
            from_sibling(eg, d, cols, ef_send.at[k, d], ef_recv.at[k, d])
        term = dot(eg[:, :, :, cols].reshape(rows, e_cols), w_dn[:, cols], ((1,), (1,)))
        grad_hidden = term if grad_hidden is None else grad_hidden + term
    grad_both = jnp.concatenate([grad_hidden * slope, grad_hidden * silu_val], axis=1).astype(BF16)

    o_cols = width // OUT_PARTS
    pair = []

    def pass_on(k):
        cols = pl.ds(k * o_cols, o_cols)
        pair[k].wait_recv()
        ro[:, :, cols] = (keep[core, :, :, cols].astype(F32) + pair_in[:, :, cols].astype(F32)).astype(BF16)
        for d in range(1, chips):
            copy = remote(
                ro.at[chip_at(d), :, cols], rin.at[chip, :, cols], r_send.at[k, d], r_recv.at[k, d], peer(d)
            )
            copy.start()
            sends.append(copy)
        rin[chip, :, cols] = ro[chip, :, cols]

    for k in range(OUT_PARTS):
        cols = pl.ds(k * o_cols, o_cols)
        part = dot(grad_both, w_gu[cols, :], ((1,), (1,))).astype(BF16)
        keep[:, :, :, cols] = part.reshape(CORES, chips, CAP, o_cols)
        copy = remote(
            keep.at[1 - core, :, :, cols], pair_in.at[:, :, cols], p_send.at[k], p_recv.at[k], sibling
        )
        copy.start()
        pair.append(copy)
        if k > 0:
            pass_on(k - 1)
    sends.extend(pair)

    def weights_part(k):
        cols = pl.ds(k * o_cols, o_cols)
        e_part = eg[:, :, :, cols].reshape(rows, o_cols)
        gdn[:, cols] = dot(hidden, e_part, ((0,), (0,))).astype(BF16)
        x_part = xg[:, :, :, cols].reshape(rows, o_cols)
        ggu[cols, :] = dot(x_part, grad_both, ((0,), (0,))).astype(BF16)

    weights_part(0)
    pass_on(OUT_PARTS - 1)
    for k in range(1, OUT_PARTS):
        weights_part(k)

    per = chips // flight
    for k in range(OUT_PARTS):
        cols = pl.ds(k * o_cols, o_cols)
        for d in range(1, chips):
            slot = rin.at[chip_from(d), :, cols]
            remote(slot, slot, r_send.at[k, d], r_recv.at[k, d], peer(d)).wait_recv()
        for e in range(flight):
            total = rin[e * per, :, cols].astype(F32)
            for q in range(1, per):
                total = total + rin[e * per + q, :, cols].astype(F32)
            sums[e, :, cols] = total.astype(BF16)
    for copy in sends:
        copy.wait_send()


def finish(flight, ggu, gdn, sums, sel, gi_hbm, gu_hbm, dn_hbm, gi_v, sems):
    copies = [
        pltpu.make_async_copy(ggu, gu_hbm.at[0, 0], sems.at[0]),
        pltpu.make_async_copy(gdn, dn_hbm.at[0, 0], sems.at[1]),
    ]
    for copy in copies:
        copy.start()
    total = None
    for e in range(flight):
        term = dot(sel[e].astype(BF16), sums[e], ((0,), (0,)))
        total = term if total is None else total + term
    gi_v[...] = total.astype(BF16)
    last = pltpu.make_async_copy(gi_v, gi_hbm.at[0], sems.at[2])
    last.start()
    for copy in copies + [last]:
        copy.wait()


def shards(inputs, upstream, route, prob, gate_up, down):
    sections = lax.axis_size("pipe")
    groups = lax.axis_size("expert")
    chips = groups // CORES
    flight = groups // SPLIT
    _, tokens, width = inputs.shape
    slots = route.shape[2]
    both_cols = gate_up.shape[3]
    hid = down.shape[2]
    dma = pltpu.SemaphoreType.DMA
    hbm = pl.BlockSpec(memory_space=pltpu.HBM)
    vmem = pl.BlockSpec(memory_space=pltpu.VMEM)
    kept = pltpu.VMEM
    ggu, gdn, sums, sel = pl.pallas_call(
        functools.partial(exchange, sections, chips, flight),
        out_shape=(
            kept((width, both_cols), BF16),
            kept((hid, width), BF16),
            kept((flight, CAP, width), BF16),
            kept((flight, CAP, tokens), F32),
        ),
        in_specs=[hbm] * 6,
        out_specs=(vmem,) * 4,
        scratch_shapes=[
            pltpu.VMEM((tokens, width), BF16),
            pltpu.VMEM((tokens, width), BF16),
            pltpu.VMEM((slots, tokens), jnp.int32),
            pltpu.VMEM((slots, tokens), F32),
            pltpu.VMEM((width, both_cols), BF16),
            pltpu.VMEM((hid, width), BF16),
            pltpu.VMEM((flight, CAP, tokens), F32),
            pltpu.VMEM((flight, CAP, tokens), F32),
            pltpu.VMEM((flight, CAP, width), BF16),
            pltpu.VMEM((CORES, chips, CAP, width), BF16),
            pltpu.VMEM((flight, CAP, width), BF16),
            pltpu.VMEM((flight, CAP, width), BF16),
            pltpu.VMEM((CORES, chips, CAP, width), BF16),
            pltpu.VMEM((chips, CAP, width), BF16),
            pltpu.VMEM((CORES, chips, CAP, width), BF16),
            pltpu.VMEM((chips, CAP, width), BF16),
            pltpu.VMEM((chips, CAP, width), BF16),
            dma((6,)),
            dma((2,)),
            dma((chips,)),
            dma((chips,)),
            dma((chips,)),
            dma((chips,)),
            dma((E_PARTS,)),
            dma((E_PARTS,)),
            dma((E_PARTS, chips)),
            dma((E_PARTS, chips)),
            dma((E_PARTS, chips)),
            dma((E_PARTS, chips)),
            dma((OUT_PARTS,)),
            dma((OUT_PARTS,)),
            dma((OUT_PARTS, chips)),
            dma((OUT_PARTS, chips)),
        ],
        compiler_params=pltpu.CompilerParams(
            collective_id=0, has_side_effects=True, vmem_limit_bytes=40 * 2**20
        ),
    )(*(
        pltpu.with_memory_space_constraint(a, pltpu.HBM)
        for a in (inputs, upstream, jnp.swapaxes(route, 1, 2), jnp.swapaxes(prob, 1, 2), gate_up, down)
    ))
    return pl.pallas_call(
        functools.partial(finish, flight),
        out_shape=(
            jax.ShapeDtypeStruct(inputs.shape, BF16),
            jax.ShapeDtypeStruct(gate_up.shape, BF16),
            jax.ShapeDtypeStruct(down.shape, BF16),
        ),
        in_specs=[vmem] * 4,
        out_specs=(hbm,) * 3,
        scratch_shapes=[pltpu.VMEM((tokens, width), BF16), dma((3,))],
        compiler_params=pltpu.CompilerParams(vmem_limit_bytes=16 * 2**20),
    )(ggu, gdn, sums, sel)


def solution(mesh):
    placed = (
        P("pipe", "expert", None),
        P("pipe", "expert", None),
        P("pipe", "expert", None),
        P("pipe", "expert", None),
        P("pipe", "expert", None, None),
        P("pipe", "expert", None, None),
    )
    return jax.shard_map(
        shards,
        mesh=mesh,
        in_specs=placed,
        out_specs=(
            P("pipe", "expert", None),
            P("pipe", "expert", None, None),
            P("pipe", "expert", None, None),
        ),
        check_vma=False,
    )
```

```python
import functools

import jax
import jax.numpy as jnp
from jax import lax
from jax.experimental import pallas as pl
from jax.experimental.pallas import tpu as pltpu
from jax.sharding import PartitionSpec as P

SPLIT = 8
CAP = 8
CORES = 2
E_PARTS = 2
OUT_PARTS = 2
W_PARTS = 4
MESH = pl.DeviceIdType.MESH
F32 = jnp.float32
BF16 = jnp.bfloat16


def dot(a, b, dims):
    return lax.dot_general(a, b, (dims, ((), ())), preferred_element_type=F32)


def remote(src, dst, send, recv, target):
    return pltpu.make_async_remote_copy(
        src_ref=src, dst_ref=dst, send_sem=send, recv_sem=recv, device_id=target, device_id_type=MESH
    )


def exchange(
    sections, chips, flight,
    x_hbm, u_hbm, route_hbm, prob_hbm, gu_hbm, dn_hbm,
    ggu, gdn, sums, sel_out,
    x_v, u_v, route_v, prob_v, w_gu, w_dn,
    s_out, s_in, xb, xg, eb, er, eg, pair_in, keep, ro, rin,
    local, s_sem, x_send, x_recv, xf_send, xf_recv,
    z_send, z_recv, e_send, e_recv, ef_send, ef_recv,
    p_send, p_recv, r_send, r_recv,
):
    section = lax.axis_index("pipe")
    me = lax.axis_index("expert")
    chip, core = me // CORES, me % CORES
    mine = me // SPLIT
    sibling = {"expert": me + 1 - 2 * core}
    ahead = {"pipe": (section + 1) % sections}
    behind = {"pipe": (section + sections - 1) % sections}
    width = x_v.shape[1]
    tokens = x_v.shape[0]
    hid = w_dn.shape[0]

    def chip_at(d):
        at, bit = 0, 1
        while bit < chips:
            at = at + (chip // bit + d // bit) % 2 * bit
            bit *= 2
        return at

    def peer(d):
        return {"expert": chip_at(d) * CORES + core}

    loads = [
        pltpu.make_async_copy(src, dst, local.at[k])
        for k, (src, dst) in enumerate(
            (
                (route_hbm.at[0], route_v),
                (prob_hbm.at[0], prob_v),
                (x_hbm.at[0], x_v),
                (u_hbm.at[0], u_v),
                (gu_hbm.at[0, 0], w_gu),
                (dn_hbm.at[0, 0], w_dn),
            )
        )
    ]
    loads[0].start()
    loads[1].start()
    barrier = pltpu.get_barrier_semaphore()
    for target in [ahead, behind, sibling] + [peer(d) for d in range(1, chips)]:
        pl.semaphore_signal(barrier, inc=1, device_id=target, device_id_type=MESH)
    loads[2].start()
    loads[3].start()
    loads[0].wait()
    loads[1].wait()
    before = (
        lax.broadcasted_iota(jnp.int32, (tokens, tokens), 0)
        < lax.broadcasted_iota(jnp.int32, (tokens, tokens), 1)
    ).astype(F32).astype(BF16)
    slots = lax.broadcasted_iota(jnp.int32, (CAP, tokens), 0).astype(F32)
    picks = []
    for e in range(flight):
        hit = route_v[...] == e
        member = jnp.max(jnp.where(hit, 1.0, 0.0), axis=0, keepdims=True)
        weight = jnp.sum(jnp.where(hit, prob_v[...], 0.0), axis=0, keepdims=True)
        member = jnp.broadcast_to(member, (CAP, tokens))
        rank = dot(member.astype(BF16), before, ((1,), (0,)))
        chosen = jnp.where((member > 0.0) & (rank == slots), 1.0, 0.0)
        sel_out[e] = chosen
        s_out[e] = chosen * weight
        picks.append(chosen.astype(BF16))
    pl.semaphore_wait(barrier, chips + 2)

    send_s = remote(s_out, s_in, s_sem.at[0], s_sem.at[1], ahead)
    send_s.start()
    sends = [send_s]

    loads[2].wait()
    loads[5].start()
    loads[4].start()
    for e in range(flight):
        xb[e] = dot(picks[e], x_v[...], ((1,), (0,))).astype(BF16)
    for d in range(1, chips):
        copy = remote(
            xb.at[chip_at(d) * CORES // SPLIT], xg.at[d, core], x_send.at[d], x_recv.at[d], peer(d)
        )
        copy.start()
        sends.append(copy)
    copy = remote(xb.at[mine], xg.at[0, core], xf_send.at[0], xf_recv.at[0], sibling)
    copy.start()
    sends.append(copy)
    xg[0, core] = xb[mine]

    loads[3].wait()
    send_s.wait_recv()
    e_cols = width // E_PARTS
    scales, gpicks = [], []
    for e in range(flight):
        weights = s_in[e]
        scales.append(jnp.sum(weights, axis=1, keepdims=True))
        gpicks.append(jnp.where(weights > 0.0, 1.0, 0.0).astype(BF16))
    z_copies = []
    for k in range(E_PARTS):
        cols = pl.ds(k * e_cols, e_cols)
        for e in range(flight):
            eb[e, :, cols] = (dot(gpicks[e], u_v[:, cols], ((1,), (0,))) * scales[e]).astype(BF16)
        copy = remote(eb.at[:, :, cols], er.at[:, :, cols], z_send.at[k], z_recv.at[k], behind)
        copy.start()
        z_copies.append(copy)
    sends.extend(z_copies)

    def relay(buf, d, cols, recv, f_send, f_recv):
        slot = buf.at[d, core, :, cols]
        remote(slot, slot, f_send, recv, sibling).wait_recv()
        copy = remote(slot, slot, f_send, f_recv, sibling)
        copy.start()
        sends.append(copy)

    def from_sibling(buf, d, cols, f_send, f_recv):
        slot = buf.at[d, 1 - core, :, cols]
        remote(slot, slot, f_send, f_recv, sibling).wait_recv()

    def send_e(k, d):
        cols = pl.ds(k * e_cols, e_cols)
        copy = remote(
            er.at[chip_at(d) * CORES // SPLIT, :, cols],
            eg.at[d, core, :, cols],
            e_send.at[k, d],
            e_recv.at[k, d],
            peer(d),
        )
        copy.start()
        sends.append(copy)

    near = chips - chips // 4
    groups = ((0, near), (near, chips))
    every = pl.ds(0, width)
    for d in range(1, chips):
        relay(xg, d, every, x_recv.at[d], xf_send.at[d], xf_recv.at[d])
    for k in range(E_PARTS):
        cols = pl.ds(k * e_cols, e_cols)
        z_copies[k].wait_recv()
        for d in range(1, near):
            send_e(k, d)
        copy = remote(
            er.at[mine, :, cols], eg.at[0, core, :, cols], ef_send.at[k, 0], ef_recv.at[k, 0], sibling
        )
        copy.start()
        sends.append(copy)
        eg[0, core, :, cols] = er[mine, :, cols]
    for k in range(E_PARTS):
        for d in range(near, chips):
            send_e(k, d)
    for d in range(chips):
        from_sibling(xg, d, every, xf_send.at[d], xf_recv.at[d])
    rows = CORES * chips * CAP
    loads[4].wait()
    both = dot(xg[...].reshape(rows, width), w_gu[...], ((1,), (0,)))
    pre_gate = both[:, :hid]
    pre_up = both[:, hid:]
    sigma = jax.nn.sigmoid(pre_gate)
    silu_val = pre_gate * sigma
    hidden = (silu_val * pre_up).astype(BF16)
    slope = pre_up * sigma * (1.0 + pre_gate * (1.0 - sigma))

    loads[5].wait()
    o_cols = width // OUT_PARTS
    pair = {}

    def relay_group(g):
        for k in range(E_PARTS):
            cols = pl.ds(k * e_cols, e_cols)
            for d in range(max(groups[g][0], 1), groups[g][1]):
                relay(eg, d, cols, e_recv.at[k, d], ef_send.at[k, d], ef_recv.at[k, d])

    def hidden_grads(g):
        first, last = groups[g]
        own = slice(first * CORES * CAP, last * CORES * CAP)
        grad_hidden = None
        for k in range(E_PARTS):
            cols = pl.ds(k * e_cols, e_cols)
            for d in range(first, last):
                from_sibling(eg, d, cols, ef_send.at[k, d], ef_recv.at[k, d])
            e_part = eg[first:last, :, :, cols].reshape((last - first) * CORES * CAP, e_cols)
            term = dot(e_part, w_dn[:, cols], ((1,), (1,)))
            grad_hidden = term if grad_hidden is None else grad_hidden + term
        return jnp.concatenate([grad_hidden * slope[own], grad_hidden * silu_val[own]], axis=1).astype(BF16)

    def to_pair(g, grads):
        first, last = groups[g]
        for k in range(OUT_PARTS):
            cols = pl.ds(k * o_cols, o_cols)
            part = dot(grads, w_gu[cols, :], ((1,), (1,))).astype(BF16)
            keep[first:last, :, :, cols] = part.reshape(last - first, CORES, CAP, o_cols)
            copy = remote(
                keep.at[first:last, 1 - core, :, cols],
                pair_in.at[first:last, :, cols],
                p_send.at[g, k],
                p_recv.at[g, k],
                sibling,
            )
            copy.start()
            pair[g, k] = copy
            sends.append(copy)

    def pass_on(g):
        first, last = groups[g]
        for k in range(OUT_PARTS):
            cols = pl.ds(k * o_cols, o_cols)
            pair[g, k].wait_recv()
            ro[first:last, :, cols] = (
                keep[first:last, core, :, cols].astype(F32) + pair_in[first:last, :, cols].astype(F32)
            ).astype(BF16)
            for d in range(max(first, 1), last):
                copy = remote(
                    ro.at[d, :, cols], rin.at[chip, :, cols], r_send.at[k, d], r_recv.at[k, d], peer(d)
                )
                copy.start()
                sends.append(copy)
            if first == 0:
                rin[chip, :, cols] = ro[0, :, cols]

    relay_group(0)
    near_grads = hidden_grads(0)
    to_pair(0, near_grads)
    relay_group(1)
    pass_on(0)
    far_grads = hidden_grads(1)
    to_pair(1, far_grads)
    grad_both = jnp.concatenate([near_grads, far_grads], axis=0)
    w_cols = width // W_PARTS

    def weights_part(k):
        cols = pl.ds(k * w_cols, w_cols)
        e_part = eg[:, :, :, cols].reshape(rows, w_cols)
        gdn[:, cols] = dot(hidden, e_part, ((0,), (0,))).astype(BF16)
        x_part = xg[:, :, :, cols].reshape(rows, w_cols)
        ggu[cols, :] = dot(x_part, grad_both, ((0,), (0,))).astype(BF16)

    weights_part(0)
    pass_on(1)
    for k in range(1, W_PARTS):
        weights_part(k)

    per = chips // flight
    for k in range(OUT_PARTS):
        cols = pl.ds(k * o_cols, o_cols)
        for d in range(1, chips):
            slot = rin.at[chip_at(d), :, cols]
            remote(slot, slot, r_send.at[k, d], r_recv.at[k, d], peer(d)).wait_recv()
        for e in range(flight):
            total = rin[e * per, :, cols].astype(F32)
            for q in range(1, per):
                total = total + rin[e * per + q, :, cols].astype(F32)
            sums[e, :, cols] = total.astype(BF16)
    for copy in sends:
        copy.wait_send()


def finish(flight, ggu, gdn, sums, sel, gi_hbm, gu_hbm, dn_hbm, gi_v, sems):
    copies = [
        pltpu.make_async_copy(ggu, gu_hbm.at[0, 0], sems.at[0]),
        pltpu.make_async_copy(gdn, dn_hbm.at[0, 0], sems.at[1]),
    ]
    for copy in copies:
        copy.start()
    total = None
    for e in range(flight):
        term = dot(sel[e].astype(BF16), sums[e], ((0,), (0,)))
        total = term if total is None else total + term
    gi_v[...] = total.astype(BF16)
    last = pltpu.make_async_copy(gi_v, gi_hbm.at[0], sems.at[2])
    last.start()
    for copy in copies + [last]:
        copy.wait()


def shards(inputs, upstream, route, prob, gate_up, down):
    sections = lax.axis_size("pipe")
    groups = lax.axis_size("expert")
    chips = groups // CORES
    flight = groups // SPLIT
    _, tokens, width = inputs.shape
    slots = route.shape[2]
    both_cols = gate_up.shape[3]
    hid = down.shape[2]
    dma = pltpu.SemaphoreType.DMA
    hbm = pl.BlockSpec(memory_space=pltpu.HBM)
    vmem = pl.BlockSpec(memory_space=pltpu.VMEM)
    kept = pltpu.VMEM
    ggu, gdn, sums, sel = pl.pallas_call(
        functools.partial(exchange, sections, chips, flight),
        out_shape=(
            kept((width, both_cols), BF16),
            kept((hid, width), BF16),
            kept((flight, CAP, width), BF16),
            kept((flight, CAP, tokens), F32),
        ),
        in_specs=[hbm] * 6,
        out_specs=(vmem,) * 4,
        scratch_shapes=[
            pltpu.VMEM((tokens, width), BF16),
            pltpu.VMEM((tokens, width), BF16),
            pltpu.VMEM((slots, tokens), jnp.int32),
            pltpu.VMEM((slots, tokens), F32),
            pltpu.VMEM((width, both_cols), BF16),
            pltpu.VMEM((hid, width), BF16),
            pltpu.VMEM((flight, CAP, tokens), F32),
            pltpu.VMEM((flight, CAP, tokens), F32),
            pltpu.VMEM((flight, CAP, width), BF16),
            pltpu.VMEM((chips, CORES, CAP, width), BF16),
            pltpu.VMEM((flight, CAP, width), BF16),
            pltpu.VMEM((flight, CAP, width), BF16),
            pltpu.VMEM((chips, CORES, CAP, width), BF16),
            pltpu.VMEM((chips, CAP, width), BF16),
            pltpu.VMEM((chips, CORES, CAP, width), BF16),
            pltpu.VMEM((chips, CAP, width), BF16),
            pltpu.VMEM((chips, CAP, width), BF16),
            dma((6,)),
            dma((2,)),
            dma((chips,)),
            dma((chips,)),
            dma((chips,)),
            dma((chips,)),
            dma((E_PARTS,)),
            dma((E_PARTS,)),
            dma((E_PARTS, chips)),
            dma((E_PARTS, chips)),
            dma((E_PARTS, chips)),
            dma((E_PARTS, chips)),
            dma((2, OUT_PARTS)),
            dma((2, OUT_PARTS)),
            dma((OUT_PARTS, chips)),
            dma((OUT_PARTS, chips)),
        ],
        compiler_params=pltpu.CompilerParams(
            collective_id=0, has_side_effects=True, vmem_limit_bytes=40 * 2**20
        ),
    )(*(
        pltpu.with_memory_space_constraint(a, pltpu.HBM)
        for a in (inputs, upstream, jnp.swapaxes(route, 1, 2), jnp.swapaxes(prob, 1, 2), gate_up, down)
    ))
    return pl.pallas_call(
        functools.partial(finish, flight),
        out_shape=(
            jax.ShapeDtypeStruct(inputs.shape, BF16),
            jax.ShapeDtypeStruct(gate_up.shape, BF16),
            jax.ShapeDtypeStruct(down.shape, BF16),
        ),
        in_specs=[vmem] * 4,
        out_specs=(hbm,) * 3,
        scratch_shapes=[pltpu.VMEM((tokens, width), BF16), dma((3,))],
        compiler_params=pltpu.CompilerParams(vmem_limit_bytes=16 * 2**20),
    )(ggu, gdn, sums, sel)


def solution(mesh):
    placed = (
        P("pipe", "expert", None),
        P("pipe", "expert", None),
        P("pipe", "expert", None),
        P("pipe", "expert", None),
        P("pipe", "expert", None, None),
        P("pipe", "expert", None, None),
    )
    return jax.shard_map(
        shards,
        mesh=mesh,
        in_specs=placed,
        out_specs=(
            P("pipe", "expert", None),
            P("pipe", "expert", None, None),
            P("pipe", "expert", None, None),
        ),
        check_vma=False,
    )
```

```python
import functools

import jax
import jax.numpy as jnp
from jax import lax
from jax.experimental import pallas as pl
from jax.experimental.pallas import tpu as pltpu
from jax.sharding import PartitionSpec as P

SPLIT = 8
CAP = 8
CORES = 2
E_PARTS = 2
OUT_PARTS = 2
W_PARTS = 4
TURN_PARTS = 8
GROUPS = 1
MESH = pl.DeviceIdType.MESH
F32 = jnp.float32
BF16 = jnp.bfloat16


def dot(a, b, dims):
    return lax.dot_general(a, b, (dims, ((), ())), preferred_element_type=F32)


def remote(src, dst, send, recv, target):
    return pltpu.make_async_remote_copy(
        src_ref=src, dst_ref=dst, send_sem=send, recv_sem=recv, device_id=target, device_id_type=MESH
    )


def exchange(
    sections, chips, flight,
    x_hbm, u_hbm, route_hbm, prob_hbm, gu_hbm, dn_hbm,
    ggu, gdn, sums, sel_out,
    x_v, u_v, route_v, prob_v, w_gu, w_dn, w_gu_t, w_dn_t, x_t,
    s_out, s_in, xb, xg, eb, er, eg, pair_in, keep, ro, rin,
    local, s_sem, x_send, x_recv, xf_send, xf_recv,
    z_send, z_recv, e_send, e_recv, ef_send, ef_recv,
    p_send, p_recv, r_send, r_recv,
):
    section = lax.axis_index("pipe")
    me = lax.axis_index("expert")
    chip, core = me // CORES, me % CORES
    mine = me // SPLIT
    sibling = {"expert": me + 1 - 2 * core}
    ahead = {"pipe": (section + 1) % sections}
    behind = {"pipe": (section + sections - 1) % sections}
    width = x_v.shape[1]
    tokens = x_v.shape[0]
    hid = w_dn.shape[0]

    def chip_at(d):
        at, bit = 0, 1
        while bit < chips:
            at = at + (chip // bit + d // bit) % 2 * bit
            bit *= 2
        return at

    def peer(d):
        return {"expert": chip_at(d) * CORES + core}

    loads = [
        pltpu.make_async_copy(src, dst, local.at[k])
        for k, (src, dst) in enumerate(
            (
                (route_hbm.at[0], route_v),
                (prob_hbm.at[0], prob_v),
                (x_hbm.at[0], x_v),
                (u_hbm.at[0], u_v),
                (gu_hbm.at[0, 0], w_gu),
                (dn_hbm.at[0, 0], w_dn),
            )
        )
    ]
    loads[0].start()
    loads[1].start()
    barrier = pltpu.get_barrier_semaphore()
    for target in [ahead, behind, sibling] + [peer(d) for d in range(1, chips)]:
        pl.semaphore_signal(barrier, inc=1, device_id=target, device_id_type=MESH)
    loads[2].start()
    loads[3].start()
    loads[0].wait()
    loads[1].wait()
    before = (
        lax.broadcasted_iota(jnp.int32, (tokens, tokens), 0)
        < lax.broadcasted_iota(jnp.int32, (tokens, tokens), 1)
    ).astype(F32).astype(BF16)
    slots = lax.broadcasted_iota(jnp.int32, (CAP, tokens), 0).astype(F32)
    picks = []
    for e in range(flight):
        hit = route_v[...] == e
        member = jnp.max(jnp.where(hit, 1.0, 0.0), axis=0, keepdims=True)
        weight = jnp.sum(jnp.where(hit, prob_v[...], 0.0), axis=0, keepdims=True)
        member = jnp.broadcast_to(member, (CAP, tokens))
        rank = dot(member.astype(BF16), before, ((1,), (0,)))
        chosen = jnp.where((member > 0.0) & (rank == slots), 1.0, 0.0)
        sel_out[e] = chosen
        s_out[e] = chosen * weight
        picks.append(chosen.astype(BF16))
    pl.semaphore_wait(barrier, chips + 2)

    send_s = remote(s_out, s_in, s_sem.at[0], s_sem.at[1], ahead)
    send_s.start()
    sends = [send_s]

    loads[2].wait()
    loads[5].start()
    loads[4].start()
    for e in range(flight):
        xb[e] = dot(picks[e], x_v[...], ((1,), (0,))).astype(BF16)
    for d in range(1, chips):
        copy = remote(
            xb.at[chip_at(d) * CORES // SPLIT], xg.at[d, core], x_send.at[d], x_recv.at[d], peer(d)
        )
        copy.start()
        sends.append(copy)
    copy = remote(xb.at[mine], xg.at[0, core], xf_send.at[0], xf_recv.at[0], sibling)
    copy.start()
    sends.append(copy)
    xg[0, core] = xb[mine]

    loads[3].wait()
    send_s.wait_recv()
    e_cols = width // E_PARTS
    scales, gpicks = [], []
    for e in range(flight):
        weights = s_in[e]
        scales.append(jnp.sum(weights, axis=1, keepdims=True))
        gpicks.append(jnp.where(weights > 0.0, 1.0, 0.0).astype(BF16))
    z_copies = []
    for k in range(E_PARTS):
        cols = pl.ds(k * e_cols, e_cols)
        for e in range(flight):
            eb[e, :, cols] = (dot(gpicks[e], u_v[:, cols], ((1,), (0,))) * scales[e]).astype(BF16)
        copy = remote(eb.at[:, :, cols], er.at[:, :, cols], z_send.at[k], z_recv.at[k], behind)
        copy.start()
        z_copies.append(copy)
    sends.extend(z_copies)

    def relay(buf, d, cols, recv, f_send, f_recv):
        slot = buf.at[d, core, :, cols]
        remote(slot, slot, f_send, recv, sibling).wait_recv()
        copy = remote(slot, slot, f_send, f_recv, sibling)
        copy.start()
        sends.append(copy)

    def from_sibling(buf, d, cols, f_send, f_recv):
        slot = buf.at[d, 1 - core, :, cols]
        remote(slot, slot, f_send, f_recv, sibling).wait_recv()

    def send_e(k, d):
        cols = pl.ds(k * e_cols, e_cols)
        copy = remote(
            er.at[chip_at(d) * CORES // SPLIT, :, cols],
            eg.at[d, core, :, cols],
            e_send.at[k, d],
            e_recv.at[k, d],
            peer(d),
        )
        copy.start()
        sends.append(copy)

    near = chips if GROUPS == 1 else chips - chips // 4
    groups = ((0, near), (near, chips))[:GROUPS]
    every = pl.ds(0, width)
    t_cols = width // TURN_PARTS
    loads[5].wait()
    for k in range(TURN_PARTS):
        cols = pl.ds(k * t_cols, t_cols)
        w_dn_t[cols, :] = w_dn[:, cols].T
    for d in range(1, chips):
        relay(xg, d, every, x_recv.at[d], xf_send.at[d], xf_recv.at[d])
    loads[4].wait()
    for k in range(TURN_PARTS // 2):
        cols = pl.ds(k * t_cols, t_cols)
        w_gu_t[:, cols] = w_gu[cols, :].T
    for k in range(E_PARTS):
        cols = pl.ds(k * e_cols, e_cols)
        z_copies[k].wait_recv()
        for d in range(1, near):
            send_e(k, d)
        copy = remote(
            er.at[mine, :, cols], eg.at[0, core, :, cols], ef_send.at[k, 0], ef_recv.at[k, 0], sibling
        )
        copy.start()
        sends.append(copy)
        eg[0, core, :, cols] = er[mine, :, cols]
    for k in range(E_PARTS):
        for d in range(near, chips):
            send_e(k, d)
    for d in range(chips):
        from_sibling(xg, d, every, xf_send.at[d], xf_recv.at[d])
    rows = CORES * chips * CAP
    both = dot(xg[...].reshape(rows, width), w_gu[...], ((1,), (0,)))
    pre_gate = both[:, :hid]
    pre_up = both[:, hid:]
    sigma = jax.nn.sigmoid(pre_gate)
    silu_val = pre_gate * sigma
    hidden = (silu_val * pre_up).astype(BF16)
    slope = pre_up * sigma * (1.0 + pre_gate * (1.0 - sigma))

    o_cols = width // OUT_PARTS
    pair = {}
    for k in range(TURN_PARTS // 2, TURN_PARTS):
        cols = pl.ds(k * t_cols, t_cols)
        w_gu_t[:, cols] = w_gu[cols, :].T
    for k in range(TURN_PARTS):
        cols = pl.ds(k * t_cols, t_cols)
        x_t[cols, :] = xg[:, :, :, cols].reshape(rows, t_cols).T

    def relay_group(g):
        for k in range(E_PARTS):
            cols = pl.ds(k * e_cols, e_cols)
            for d in range(max(groups[g][0], 1), groups[g][1]):
                relay(eg, d, cols, e_recv.at[k, d], ef_send.at[k, d], ef_recv.at[k, d])

    def hidden_grads(g):
        first, last = groups[g]
        own = slice(first * CORES * CAP, last * CORES * CAP)
        grad_hidden = None
        for k in range(E_PARTS):
            cols = pl.ds(k * e_cols, e_cols)
            for d in range(first, last):
                from_sibling(eg, d, cols, ef_send.at[k, d], ef_recv.at[k, d])
            e_part = eg[first:last, :, :, cols].reshape((last - first) * CORES * CAP, e_cols)
            term = dot(e_part, w_dn_t[cols, :], ((1,), (0,)))
            grad_hidden = term if grad_hidden is None else grad_hidden + term
        return jnp.concatenate([grad_hidden * slope[own], grad_hidden * silu_val[own]], axis=1).astype(BF16)

    def to_pair(g, grads):
        first, last = groups[g]
        for k in range(OUT_PARTS):
            cols = pl.ds(k * o_cols, o_cols)
            part = dot(grads, w_gu_t[:, cols], ((1,), (0,))).astype(BF16)
            keep[first:last, :, :, cols] = part.reshape(last - first, CORES, CAP, o_cols)
            copy = remote(
                keep.at[first:last, 1 - core, :, cols],
                pair_in.at[first:last, :, cols],
                p_send.at[g, k],
                p_recv.at[g, k],
                sibling,
            )
            copy.start()
            pair[g, k] = copy
            sends.append(copy)

    def pass_on(g):
        first, last = groups[g]
        for k in range(OUT_PARTS):
            cols = pl.ds(k * o_cols, o_cols)
            pair[g, k].wait_recv()
            ro[first:last, :, cols] = (
                keep[first:last, core, :, cols].astype(F32) + pair_in[first:last, :, cols].astype(F32)
            ).astype(BF16)
            for d in range(max(first, 1), last):
                copy = remote(
                    ro.at[d, :, cols], rin.at[chip, :, cols], r_send.at[k, d], r_recv.at[k, d], peer(d)
                )
                copy.start()
                sends.append(copy)
            if first == 0:
                rin[chip, :, cols] = ro[0, :, cols]

    grads = []
    for g in range(GROUPS):
        relay_group(g)
        if g > 0:
            pass_on(g - 1)
        grads.append(hidden_grads(g))
        to_pair(g, grads[g])
    grad_both = jnp.concatenate(grads, axis=0) if GROUPS > 1 else grads[0]
    w_cols = width // W_PARTS

    def weights_part(k):
        cols = pl.ds(k * w_cols, w_cols)
        e_part = eg[:, :, :, cols].reshape(rows, w_cols)
        gdn[:, cols] = dot(hidden, e_part, ((0,), (0,))).astype(BF16)
        ggu[cols, :] = dot(x_t[cols, :], grad_both, ((1,), (0,))).astype(BF16)

    weights_part(0)
    pass_on(GROUPS - 1)
    for k in range(1, W_PARTS):
        weights_part(k)

    per = chips // flight
    for k in range(OUT_PARTS):
        cols = pl.ds(k * o_cols, o_cols)
        for d in range(1, chips):
            slot = rin.at[chip_at(d), :, cols]
            remote(slot, slot, r_send.at[k, d], r_recv.at[k, d], peer(d)).wait_recv()
        for e in range(flight):
            total = rin[e * per, :, cols].astype(F32)
            for q in range(1, per):
                total = total + rin[e * per + q, :, cols].astype(F32)
            sums[e, :, cols] = total.astype(BF16)
    for copy in sends:
        copy.wait_send()


def finish(flight, ggu, gdn, sums, sel, gi_hbm, gu_hbm, dn_hbm, gi_v, sems):
    copies = [
        pltpu.make_async_copy(ggu, gu_hbm.at[0, 0], sems.at[0]),
        pltpu.make_async_copy(gdn, dn_hbm.at[0, 0], sems.at[1]),
    ]
    for copy in copies:
        copy.start()
    total = None
    for e in range(flight):
        term = dot(sel[e].astype(BF16), sums[e], ((0,), (0,)))
        total = term if total is None else total + term
    gi_v[...] = total.astype(BF16)
    last = pltpu.make_async_copy(gi_v, gi_hbm.at[0], sems.at[2])
    last.start()
    for copy in copies + [last]:
        copy.wait()


def shards(inputs, upstream, route, prob, gate_up, down):
    sections = lax.axis_size("pipe")
    groups = lax.axis_size("expert")
    chips = groups // CORES
    flight = groups // SPLIT
    _, tokens, width = inputs.shape
    slots = route.shape[2]
    both_cols = gate_up.shape[3]
    hid = down.shape[2]
    dma = pltpu.SemaphoreType.DMA
    hbm = pl.BlockSpec(memory_space=pltpu.HBM)
    vmem = pl.BlockSpec(memory_space=pltpu.VMEM)
    kept = pltpu.VMEM
    ggu, gdn, sums, sel = pl.pallas_call(
        functools.partial(exchange, sections, chips, flight),
        out_shape=(
            kept((width, both_cols), BF16),
            kept((hid, width), BF16),
            kept((flight, CAP, width), BF16),
            kept((flight, CAP, tokens), F32),
        ),
        in_specs=[hbm] * 6,
        out_specs=(vmem,) * 4,
        scratch_shapes=[
            pltpu.VMEM((tokens, width), BF16),
            pltpu.VMEM((tokens, width), BF16),
            pltpu.VMEM((slots, tokens), jnp.int32),
            pltpu.VMEM((slots, tokens), F32),
            pltpu.VMEM((width, both_cols), BF16),
            pltpu.VMEM((hid, width), BF16),
            pltpu.VMEM((both_cols, width), BF16),
            pltpu.VMEM((width, hid), BF16),
            pltpu.VMEM((width, groups * CAP), BF16),
            pltpu.VMEM((flight, CAP, tokens), F32),
            pltpu.VMEM((flight, CAP, tokens), F32),
            pltpu.VMEM((flight, CAP, width), BF16),
            pltpu.VMEM((chips, CORES, CAP, width), BF16),
            pltpu.VMEM((flight, CAP, width), BF16),
            pltpu.VMEM((flight, CAP, width), BF16),
            pltpu.VMEM((chips, CORES, CAP, width), BF16),
            pltpu.VMEM((chips, CAP, width), BF16),
            pltpu.VMEM((chips, CORES, CAP, width), BF16),
            pltpu.VMEM((chips, CAP, width), BF16),
            pltpu.VMEM((chips, CAP, width), BF16),
            dma((6,)),
            dma((2,)),
            dma((chips,)),
            dma((chips,)),
            dma((chips,)),
            dma((chips,)),
            dma((E_PARTS,)),
            dma((E_PARTS,)),
            dma((E_PARTS, chips)),
            dma((E_PARTS, chips)),
            dma((E_PARTS, chips)),
            dma((E_PARTS, chips)),
            dma((GROUPS, OUT_PARTS)),
            dma((GROUPS, OUT_PARTS)),
            dma((OUT_PARTS, chips)),
            dma((OUT_PARTS, chips)),
        ],
        compiler_params=pltpu.CompilerParams(
            collective_id=0, has_side_effects=True, vmem_limit_bytes=40 * 2**20
        ),
    )(*(
        pltpu.with_memory_space_constraint(a, pltpu.HBM)
        for a in (inputs, upstream, jnp.swapaxes(route, 1, 2), jnp.swapaxes(prob, 1, 2), gate_up, down)
    ))
    return pl.pallas_call(
        functools.partial(finish, flight),
        out_shape=(
            jax.ShapeDtypeStruct(inputs.shape, BF16),
            jax.ShapeDtypeStruct(gate_up.shape, BF16),
            jax.ShapeDtypeStruct(down.shape, BF16),
        ),
        in_specs=[vmem] * 4,
        out_specs=(hbm,) * 3,
        scratch_shapes=[pltpu.VMEM((tokens, width), BF16), dma((3,))],
        compiler_params=pltpu.CompilerParams(vmem_limit_bytes=16 * 2**20),
    )(ggu, gdn, sums, sel)


def solution(mesh):
    placed = (
        P("pipe", "expert", None),
        P("pipe", "expert", None),
        P("pipe", "expert", None),
        P("pipe", "expert", None),
        P("pipe", "expert", None, None),
        P("pipe", "expert", None, None),
    )
    return jax.shard_map(
        shards,
        mesh=mesh,
        in_specs=placed,
        out_specs=(
            P("pipe", "expert", None),
            P("pipe", "expert", None, None),
            P("pipe", "expert", None, None),
        ),
        check_vma=False,
    )
```

```python
import functools

import jax
import jax.numpy as jnp
from jax import lax
from jax.experimental import pallas as pl
from jax.experimental.pallas import tpu as pltpu
from jax.sharding import PartitionSpec as P

SPLIT = 8
CAP = 8
CORES = 2
E_PARTS = 2
OUT_PARTS = 4
W_PARTS = 4
TURN_PARTS = 4
MESH = pl.DeviceIdType.MESH
F32 = jnp.float32
BF16 = jnp.bfloat16


def dot(a, b, dims):
    return lax.dot_general(a, b, (dims, ((), ())), preferred_element_type=F32)


def remote(src, dst, send, recv, target):
    return pltpu.make_async_remote_copy(
        src_ref=src, dst_ref=dst, send_sem=send, recv_sem=recv, device_id=target, device_id_type=MESH
    )


def exchange(
    sections, chips, flight,
    x_hbm, u_hbm, route_hbm, prob_hbm, gu_hbm, dn_hbm,
    ggu, gdn, sums, sel_out,
    x_v, u_v, route_v, prob_v, w_gu, w_dn, x_t,
    s_out, s_in, xb, xg, eb, er, eg, pair_in, keep, ro, rin,
    local, s_sem, x_send, x_recv, xf_send, xf_recv,
    z_send, z_recv, e_send, e_recv, ef_send, ef_recv,
    p_send, p_recv, r_send, r_recv,
):
    section = lax.axis_index("pipe")
    me = lax.axis_index("expert")
    chip, core = me // CORES, me % CORES
    mine = me // SPLIT
    sibling = {"expert": me + 1 - 2 * core}
    ahead = {"pipe": (section + 1) % sections}
    behind = {"pipe": (section + sections - 1) % sections}
    width = x_v.shape[1]
    tokens = x_v.shape[0]
    hid = w_dn.shape[0]

    def chip_at(d):
        at, bit = 0, 1
        while bit < chips:
            at = at + (chip // bit + d // bit) % 2 * bit
            bit *= 2
        return at

    def peer(d):
        return {"expert": chip_at(d) * CORES + core}

    loads = [
        pltpu.make_async_copy(src, dst, local.at[k])
        for k, (src, dst) in enumerate(
            (
                (route_hbm.at[0], route_v),
                (prob_hbm.at[0], prob_v),
                (x_hbm.at[0], x_v),
                (u_hbm.at[0], u_v),
                (gu_hbm.at[0, 0], w_gu),
                (dn_hbm.at[0, 0], w_dn),
            )
        )
    ]
    loads[0].start()
    loads[1].start()
    barrier = pltpu.get_barrier_semaphore()
    for target in [behind, sibling] + [peer(d) for d in range(1, chips)]:
        pl.semaphore_signal(barrier, inc=1, device_id=target, device_id_type=MESH)
    loads[2].start()
    loads[3].start()
    loads[0].wait()
    loads[1].wait()
    before = (
        lax.broadcasted_iota(jnp.int32, (tokens, tokens), 0)
        < lax.broadcasted_iota(jnp.int32, (tokens, tokens), 1)
    ).astype(F32).astype(BF16)
    slots = lax.broadcasted_iota(jnp.int32, (CAP, tokens), 0).astype(F32)
    picks = []
    for e in range(flight):
        hit = route_v[...] == e
        member = jnp.max(jnp.where(hit, 1.0, 0.0), axis=0, keepdims=True)
        weight = jnp.sum(jnp.where(hit, prob_v[...], 0.0), axis=0, keepdims=True)
        member = jnp.broadcast_to(member, (CAP, tokens))
        rank = dot(member.astype(BF16), before, ((1,), (0,)))
        chosen = jnp.where((member > 0.0) & (rank == slots), 1.0, 0.0)
        sel_out[e] = chosen
        s_out[e] = chosen * weight
        picks.append(chosen.astype(BF16))
    pl.semaphore_wait(barrier, chips + 1)

    send_s = remote(s_out, s_in, s_sem.at[0], s_sem.at[1], ahead)
    send_s.start()
    sends = [send_s]

    loads[2].wait()
    loads[5].start()
    loads[4].start()
    for e in range(flight):
        xb[e] = dot(picks[e], x_v[...], ((1,), (0,))).astype(BF16)
    for d in range(1, chips):
        copy = remote(
            xb.at[chip_at(d) * CORES // SPLIT], xg.at[d, core], x_send.at[d], x_recv.at[d], peer(d)
        )
        copy.start()
        sends.append(copy)
    copy = remote(xb.at[mine], xg.at[0, core], xf_send.at[0], xf_recv.at[0], sibling)
    copy.start()
    sends.append(copy)
    xg[0, core] = xb[mine]

    loads[3].wait()
    send_s.wait_recv()
    e_cols = width // E_PARTS
    scales, gpicks = [], []
    for e in range(flight):
        weights = s_in[e]
        scales.append(jnp.sum(weights, axis=1, keepdims=True))
        gpicks.append(jnp.where(weights > 0.0, 1.0, 0.0).astype(BF16))
    z_copies = []
    for k in range(E_PARTS):
        cols = pl.ds(k * e_cols, e_cols)
        for e in range(flight):
            eb[e, :, cols] = (dot(gpicks[e], u_v[:, cols], ((1,), (0,))) * scales[e]).astype(BF16)
        copy = remote(eb.at[:, :, cols], er.at[:, :, cols], z_send.at[k], z_recv.at[k], behind)
        copy.start()
        z_copies.append(copy)
    sends.extend(z_copies)

    def relay(buf, d, cols, recv, f_send, f_recv):
        slot = buf.at[d, core, :, cols]
        remote(slot, slot, f_send, recv, sibling).wait_recv()
        copy = remote(slot, slot, f_send, f_recv, sibling)
        copy.start()
        sends.append(copy)

    def from_sibling(buf, d, cols, f_send, f_recv):
        slot = buf.at[d, 1 - core, :, cols]
        remote(slot, slot, f_send, f_recv, sibling).wait_recv()

    def send_e(k, d):
        cols = pl.ds(k * e_cols, e_cols)
        copy = remote(
            er.at[chip_at(d) * CORES // SPLIT, :, cols],
            eg.at[d, core, :, cols],
            e_send.at[k, d],
            e_recv.at[k, d],
            peer(d),
        )
        copy.start()
        sends.append(copy)

    every = pl.ds(0, width)
    for d in range(1, chips):
        relay(xg, d, every, x_recv.at[d], xf_send.at[d], xf_recv.at[d])
    loads[4].wait()
    loads[5].wait()
    for k in range(E_PARTS):
        cols = pl.ds(k * e_cols, e_cols)
        z_copies[k].wait_recv()
        for d in range(1, chips):
            send_e(k, d)
        copy = remote(
            er.at[mine, :, cols], eg.at[0, core, :, cols], ef_send.at[k, 0], ef_recv.at[k, 0], sibling
        )
        copy.start()
        sends.append(copy)
        eg[0, core, :, cols] = er[mine, :, cols]
    for d in range(chips):
        from_sibling(xg, d, every, xf_send.at[d], xf_recv.at[d])
    rows = CORES * chips * CAP
    both = dot(xg[...].reshape(rows, width), w_gu[...], ((1,), (0,)))
    pre_gate = both[:, :hid]
    pre_up = both[:, hid:]
    sigma = jax.nn.sigmoid(pre_gate)
    silu_val = pre_gate * sigma
    hidden = (silu_val * pre_up).astype(BF16)
    slope = pre_up * sigma * (1.0 + pre_gate * (1.0 - sigma))

    o_cols = width // OUT_PARTS
    pair = {}
    t_cols = width // TURN_PARTS
    for k in range(TURN_PARTS):
        cols = pl.ds(k * t_cols, t_cols)
        x_t[cols, :] = xg[:, :, :, cols].reshape(rows, t_cols).T

    def to_pair(k):
        cols = pl.ds(k * o_cols, o_cols)
        part = dot(grad_both, w_gu[cols, :], ((1,), (1,))).astype(BF16)
        keep[:, :, :, cols] = part.reshape(chips, CORES, CAP, o_cols)
        copy = remote(
            keep.at[:, 1 - core, :, cols], pair_in.at[:, :, cols], p_send.at[k], p_recv.at[k], sibling
        )
        copy.start()
        pair[k] = copy
        sends.append(copy)

    def pass_on(k):
        cols = pl.ds(k * o_cols, o_cols)
        pair[k].wait_recv()
        ro[:, :, cols] = (keep[:, core, :, cols].astype(F32) + pair_in[:, :, cols].astype(F32)).astype(BF16)
        for d in range(1, chips):
            copy = remote(
                ro.at[d, :, cols], rin.at[chip, :, cols], r_send.at[k, d], r_recv.at[k, d], peer(d)
            )
            copy.start()
            sends.append(copy)
        rin[chip, :, cols] = ro[0, :, cols]

    for k in range(E_PARTS):
        cols = pl.ds(k * e_cols, e_cols)
        for d in range(1, chips):
            relay(eg, d, cols, e_recv.at[k, d], ef_send.at[k, d], ef_recv.at[k, d])
    grad_hidden = None
    for k in range(E_PARTS):
        cols = pl.ds(k * e_cols, e_cols)
        for d in range(chips):
            from_sibling(eg, d, cols, ef_send.at[k, d], ef_recv.at[k, d])
        term = dot(eg[:, :, :, cols].reshape(rows, e_cols), w_dn[:, cols], ((1,), (1,)))
        grad_hidden = term if grad_hidden is None else grad_hidden + term
    grad_both = jnp.concatenate([grad_hidden * slope, grad_hidden * silu_val], axis=1).astype(BF16)
    for k in range(OUT_PARTS):
        to_pair(k)
        if k > 0:
            pass_on(k - 1)
    w_cols = width // W_PARTS

    def weights_part(k):
        cols = pl.ds(k * w_cols, w_cols)
        e_part = eg[:, :, :, cols].reshape(rows, w_cols)
        gdn[:, cols] = dot(hidden, e_part, ((0,), (0,))).astype(BF16)
        ggu[cols, :] = dot(x_t[cols, :], grad_both, ((1,), (0,))).astype(BF16)

    weights_part(0)
    pass_on(OUT_PARTS - 1)
    for k in range(1, W_PARTS):
        weights_part(k)

    per = chips // flight
    for k in range(OUT_PARTS):
        cols = pl.ds(k * o_cols, o_cols)
        for d in range(1, chips):
            slot = rin.at[chip_at(d), :, cols]
            remote(slot, slot, r_send.at[k, d], r_recv.at[k, d], peer(d)).wait_recv()
        for e in range(flight):
            total = rin[e * per, :, cols].astype(F32)
            for q in range(1, per):
                total = total + rin[e * per + q, :, cols].astype(F32)
            sums[e, :, cols] = total.astype(BF16)
    for copy in sends:
        copy.wait_send()


def finish(flight, ggu, gdn, sums, sel, gi_hbm, gu_hbm, dn_hbm, gi_v, sems):
    copies = [
        pltpu.make_async_copy(ggu, gu_hbm.at[0, 0], sems.at[0]),
        pltpu.make_async_copy(gdn, dn_hbm.at[0, 0], sems.at[1]),
    ]
    for copy in copies:
        copy.start()
    total = None
    for e in range(flight):
        term = dot(sel[e].astype(BF16), sums[e], ((0,), (0,)))
        total = term if total is None else total + term
    gi_v[...] = total.astype(BF16)
    last = pltpu.make_async_copy(gi_v, gi_hbm.at[0], sems.at[2])
    last.start()
    for copy in copies + [last]:
        copy.wait()


def shards(inputs, upstream, route, prob, gate_up, down):
    sections = lax.axis_size("pipe")
    groups = lax.axis_size("expert")
    chips = groups // CORES
    flight = groups // SPLIT
    _, tokens, width = inputs.shape
    slots = route.shape[2]
    both_cols = gate_up.shape[3]
    hid = down.shape[2]
    dma = pltpu.SemaphoreType.DMA
    hbm = pl.BlockSpec(memory_space=pltpu.HBM)
    vmem = pl.BlockSpec(memory_space=pltpu.VMEM)
    kept = pltpu.VMEM
    ggu, gdn, sums, sel = pl.pallas_call(
        functools.partial(exchange, sections, chips, flight),
        out_shape=(
            kept((width, both_cols), BF16),
            kept((hid, width), BF16),
            kept((flight, CAP, width), BF16),
            kept((flight, CAP, tokens), F32),
        ),
        in_specs=[hbm] * 6,
        out_specs=(vmem,) * 4,
        scratch_shapes=[
            pltpu.VMEM((tokens, width), BF16),
            pltpu.VMEM((tokens, width), BF16),
            pltpu.VMEM((slots, tokens), jnp.int32),
            pltpu.VMEM((slots, tokens), F32),
            pltpu.VMEM((width, both_cols), BF16),
            pltpu.VMEM((hid, width), BF16),
            pltpu.VMEM((width, groups * CAP), BF16),
            pltpu.VMEM((flight, CAP, tokens), F32),
            pltpu.VMEM((flight, CAP, tokens), F32),
            pltpu.VMEM((flight, CAP, width), BF16),
            pltpu.VMEM((chips, CORES, CAP, width), BF16),
            pltpu.VMEM((flight, CAP, width), BF16),
            pltpu.VMEM((flight, CAP, width), BF16),
            pltpu.VMEM((chips, CORES, CAP, width), BF16),
            pltpu.VMEM((chips, CAP, width), BF16),
            pltpu.VMEM((chips, CORES, CAP, width), BF16),
            pltpu.VMEM((chips, CAP, width), BF16),
            pltpu.VMEM((chips, CAP, width), BF16),
            dma((6,)),
            dma((2,)),
            dma((chips,)),
            dma((chips,)),
            dma((chips,)),
            dma((chips,)),
            dma((E_PARTS,)),
            dma((E_PARTS,)),
            dma((E_PARTS, chips)),
            dma((E_PARTS, chips)),
            dma((E_PARTS, chips)),
            dma((E_PARTS, chips)),
            dma((OUT_PARTS,)),
            dma((OUT_PARTS,)),
            dma((OUT_PARTS, chips)),
            dma((OUT_PARTS, chips)),
        ],
        compiler_params=pltpu.CompilerParams(
            collective_id=0, has_side_effects=True, vmem_limit_bytes=40 * 2**20
        ),
    )(*(
        pltpu.with_memory_space_constraint(a, pltpu.HBM)
        for a in (inputs, upstream, jnp.swapaxes(route, 1, 2), jnp.swapaxes(prob, 1, 2), gate_up, down)
    ))
    return pl.pallas_call(
        functools.partial(finish, flight),
        out_shape=(
            jax.ShapeDtypeStruct(inputs.shape, BF16),
            jax.ShapeDtypeStruct(gate_up.shape, BF16),
            jax.ShapeDtypeStruct(down.shape, BF16),
        ),
        in_specs=[vmem] * 4,
        out_specs=(hbm,) * 3,
        scratch_shapes=[pltpu.VMEM((tokens, width), BF16), dma((3,))],
        compiler_params=pltpu.CompilerParams(vmem_limit_bytes=16 * 2**20),
    )(ggu, gdn, sums, sel)


def solution(mesh):
    placed = (
        P("pipe", "expert", None),
        P("pipe", "expert", None),
        P("pipe", "expert", None),
        P("pipe", "expert", None),
        P("pipe", "expert", None, None),
        P("pipe", "expert", None, None),
    )
    return jax.shard_map(
        shards,
        mesh=mesh,
        in_specs=placed,
        out_specs=(
            P("pipe", "expert", None),
            P("pipe", "expert", None, None),
            P("pipe", "expert", None, None),
        ),
        check_vma=False,
    )
```

```python
import functools

import jax
import jax.numpy as jnp
from jax import lax
from jax.experimental import pallas as pl
from jax.experimental.pallas import tpu as pltpu
from jax.sharding import PartitionSpec as P

SPLIT = 8
CAP = 8
CORES = 2
E_PARTS = 2
OUT_PARTS = 4
W_PARTS = 4
TURN_PARTS = 4
MESH = pl.DeviceIdType.MESH
F32 = jnp.float32
BF16 = jnp.bfloat16


def dot(a, b, dims):
    return lax.dot_general(a, b, (dims, ((), ())), preferred_element_type=F32)


def remote(src, dst, send, recv, target):
    return pltpu.make_async_remote_copy(
        src_ref=src, dst_ref=dst, send_sem=send, recv_sem=recv, device_id=target, device_id_type=MESH
    )


def exchange(
    sections, chips, flight,
    x_hbm, u_hbm, route_hbm, prob_hbm, gu_hbm, dn_hbm,
    ggu, gdn, sums, sel_out, x_t, grads,
    x_v, u_v, route_v, prob_v, w_gu, w_dn,
    s_out, s_in, xb, xg, eb, er, eg, pair_in, keep, ro, rin,
    local, s_sem, x_send, x_recv, xf_send, xf_recv,
    z_send, z_recv, e_send, e_recv, ef_send, ef_recv,
    p_send, p_recv, r_send, r_recv,
):
    section = lax.axis_index("pipe")
    me = lax.axis_index("expert")
    chip, core = me // CORES, me % CORES
    mine = me // SPLIT
    sibling = {"expert": me + 1 - 2 * core}
    ahead = {"pipe": (section + 1) % sections}
    behind = {"pipe": (section + sections - 1) % sections}
    width = x_v.shape[1]
    tokens = x_v.shape[0]
    hid = w_dn.shape[0]

    def chip_at(d):
        at, bit = 0, 1
        while bit < chips:
            at = at + (chip // bit + d // bit) % 2 * bit
            bit *= 2
        return at

    def peer(d):
        return {"expert": chip_at(d) * CORES + core}

    loads = [
        pltpu.make_async_copy(src, dst, local.at[k])
        for k, (src, dst) in enumerate(
            (
                (route_hbm.at[0], route_v),
                (prob_hbm.at[0], prob_v),
                (x_hbm.at[0], x_v),
                (u_hbm.at[0], u_v),
                (gu_hbm.at[0, 0], w_gu),
                (dn_hbm.at[0, 0], w_dn),
            )
        )
    ]
    loads[0].start()
    loads[1].start()
    barrier = pltpu.get_barrier_semaphore()
    for target in [behind, sibling] + [peer(d) for d in range(1, chips)]:
        pl.semaphore_signal(barrier, inc=1, device_id=target, device_id_type=MESH)
    loads[2].start()
    loads[3].start()
    loads[0].wait()
    loads[1].wait()
    before = (
        lax.broadcasted_iota(jnp.int32, (tokens, tokens), 0)
        < lax.broadcasted_iota(jnp.int32, (tokens, tokens), 1)
    ).astype(F32).astype(BF16)
    slots = lax.broadcasted_iota(jnp.int32, (CAP, tokens), 0).astype(F32)
    picks = []
    for e in range(flight):
        hit = route_v[...] == e
        member = jnp.max(jnp.where(hit, 1.0, 0.0), axis=0, keepdims=True)
        weight = jnp.sum(jnp.where(hit, prob_v[...], 0.0), axis=0, keepdims=True)
        member = jnp.broadcast_to(member, (CAP, tokens))
        rank = dot(member.astype(BF16), before, ((1,), (0,)))
        chosen = jnp.where((member > 0.0) & (rank == slots), 1.0, 0.0)
        sel_out[e] = chosen
        s_out[e] = chosen * weight
        picks.append(chosen.astype(BF16))
    pl.semaphore_wait(barrier, chips + 1)

    send_s = remote(s_out, s_in, s_sem.at[0], s_sem.at[1], ahead)
    send_s.start()
    sends = [send_s]

    loads[2].wait()
    loads[5].start()
    loads[4].start()
    for e in range(flight):
        xb[e] = dot(picks[e], x_v[...], ((1,), (0,))).astype(BF16)
    for d in range(1, chips):
        copy = remote(
            xb.at[chip_at(d) * CORES // SPLIT], xg.at[d, core], x_send.at[d], x_recv.at[d], peer(d)
        )
        copy.start()
        sends.append(copy)
    copy = remote(xb.at[mine], xg.at[0, core], xf_send.at[0], xf_recv.at[0], sibling)
    copy.start()
    sends.append(copy)
    xg[0, core] = xb[mine]

    loads[3].wait()
    send_s.wait_recv()
    e_cols = width // E_PARTS
    scales, gpicks = [], []
    for e in range(flight):
        weights = s_in[e]
        scales.append(jnp.sum(weights, axis=1, keepdims=True))
        gpicks.append(jnp.where(weights > 0.0, 1.0, 0.0).astype(BF16))
    z_copies = []
    for k in range(E_PARTS):
        cols = pl.ds(k * e_cols, e_cols)
        for e in range(flight):
            eb[e, :, cols] = (dot(gpicks[e], u_v[:, cols], ((1,), (0,))) * scales[e]).astype(BF16)
        copy = remote(eb.at[:, :, cols], er.at[:, :, cols], z_send.at[k], z_recv.at[k], behind)
        copy.start()
        z_copies.append(copy)
    sends.extend(z_copies)

    def relay(buf, d, cols, recv, f_send, f_recv):
        slot = buf.at[d, core, :, cols]
        remote(slot, slot, f_send, recv, sibling).wait_recv()
        copy = remote(slot, slot, f_send, f_recv, sibling)
        copy.start()
        sends.append(copy)

    def from_sibling(buf, d, cols, f_send, f_recv):
        slot = buf.at[d, 1 - core, :, cols]
        remote(slot, slot, f_send, f_recv, sibling).wait_recv()

    def send_e(k, d):
        cols = pl.ds(k * e_cols, e_cols)
        copy = remote(
            er.at[chip_at(d) * CORES // SPLIT, :, cols],
            eg.at[d, core, :, cols],
            e_send.at[k, d],
            e_recv.at[k, d],
            peer(d),
        )
        copy.start()
        sends.append(copy)

    every = pl.ds(0, width)
    for d in range(1, chips):
        relay(xg, d, every, x_recv.at[d], xf_send.at[d], xf_recv.at[d])
    loads[4].wait()
    loads[5].wait()
    for k in range(E_PARTS):
        cols = pl.ds(k * e_cols, e_cols)
        z_copies[k].wait_recv()
        for d in range(1, chips):
            send_e(k, d)
        copy = remote(
            er.at[mine, :, cols], eg.at[0, core, :, cols], ef_send.at[k, 0], ef_recv.at[k, 0], sibling
        )
        copy.start()
        sends.append(copy)
        eg[0, core, :, cols] = er[mine, :, cols]
    for d in range(chips):
        from_sibling(xg, d, every, xf_send.at[d], xf_recv.at[d])
    rows = CORES * chips * CAP
    both = dot(xg[...].reshape(rows, width), w_gu[...], ((1,), (0,)))
    pre_gate = both[:, :hid]
    pre_up = both[:, hid:]
    sigma = jax.nn.sigmoid(pre_gate)
    silu_val = pre_gate * sigma
    hidden = (silu_val * pre_up).astype(BF16)
    slope = pre_up * sigma * (1.0 + pre_gate * (1.0 - sigma))

    o_cols = width // OUT_PARTS
    pair = {}
    t_cols = width // TURN_PARTS
    for k in range(TURN_PARTS):
        cols = pl.ds(k * t_cols, t_cols)
        x_t[cols, :] = xg[:, :, :, cols].reshape(rows, t_cols).T

    def to_pair(k):
        cols = pl.ds(k * o_cols, o_cols)
        part = dot(grad_both, w_gu[cols, :], ((1,), (1,))).astype(BF16)
        keep[:, :, :, cols] = part.reshape(chips, CORES, CAP, o_cols)
        copy = remote(
            keep.at[:, 1 - core, :, cols], pair_in.at[:, :, cols], p_send.at[k], p_recv.at[k], sibling
        )
        copy.start()
        pair[k] = copy
        sends.append(copy)

    def pass_on(k):
        cols = pl.ds(k * o_cols, o_cols)
        pair[k].wait_recv()
        ro[:, :, cols] = (keep[:, core, :, cols].astype(F32) + pair_in[:, :, cols].astype(F32)).astype(BF16)
        for d in range(1, chips):
            copy = remote(
                ro.at[d, :, cols], rin.at[chip, :, cols], r_send.at[k, d], r_recv.at[k, d], peer(d)
            )
            copy.start()
            sends.append(copy)
        rin[chip, :, cols] = ro[0, :, cols]

    for k in range(E_PARTS):
        cols = pl.ds(k * e_cols, e_cols)
        for d in range(1, chips):
            relay(eg, d, cols, e_recv.at[k, d], ef_send.at[k, d], ef_recv.at[k, d])
    grad_hidden = None
    for k in range(E_PARTS):
        cols = pl.ds(k * e_cols, e_cols)
        for d in range(chips):
            from_sibling(eg, d, cols, ef_send.at[k, d], ef_recv.at[k, d])
        term = dot(eg[:, :, :, cols].reshape(rows, e_cols), w_dn[:, cols], ((1,), (1,)))
        grad_hidden = term if grad_hidden is None else grad_hidden + term
    grad_both = jnp.concatenate([grad_hidden * slope, grad_hidden * silu_val], axis=1).astype(BF16)
    grads[...] = grad_both
    for k in range(OUT_PARTS):
        to_pair(k)
        if k > 0:
            pass_on(k - 1)
    w_cols = width // W_PARTS

    def weights_part(k):
        cols = pl.ds(k * w_cols, w_cols)
        e_part = eg[:, :, :, cols].reshape(rows, w_cols)
        gdn[:, cols] = dot(hidden, e_part, ((0,), (0,))).astype(BF16)
        if k < W_PARTS // 2:
            ggu[cols, :] = dot(x_t[cols, :], grad_both, ((1,), (0,))).astype(BF16)

    weights_part(0)
    pass_on(OUT_PARTS - 1)
    for k in range(1, W_PARTS):
        weights_part(k)

    per = chips // flight
    for k in range(OUT_PARTS):
        cols = pl.ds(k * o_cols, o_cols)
        for d in range(1, chips):
            slot = rin.at[chip_at(d), :, cols]
            remote(slot, slot, r_send.at[k, d], r_recv.at[k, d], peer(d)).wait_recv()
        for e in range(flight):
            total = rin[e * per, :, cols].astype(F32)
            for q in range(1, per):
                total = total + rin[e * per + q, :, cols].astype(F32)
            sums[e, :, cols] = total.astype(BF16)
    for copy in sends:
        copy.wait_send()


def finish(flight, ggu, gdn, sums, sel, x_t, grads, gi_hbm, gu_hbm, dn_hbm, gi_v, ggu_v, sems):
    width = x_t.shape[0]
    half = ggu.shape[0]
    copies = []

    def write(src, dst):
        copy = pltpu.make_async_copy(src, dst, sems.at[len(copies)])
        copy.start()
        copies.append(copy)

    write(ggu, gu_hbm.at[0, 0, pl.ds(0, half), :])
    write(gdn, dn_hbm.at[0, 0])
    step = width // W_PARTS
    for k in range(W_PARTS // 2):
        rows = pl.ds(k * step, step)
        ahead = pl.ds(half + k * step, step)
        ggu_v[rows, :] = dot(x_t[ahead, :], grads[...], ((1,), (0,))).astype(BF16)
        write(ggu_v.at[rows, :], gu_hbm.at[0, 0, ahead, :])
    for k in range(2):
        cols = pl.ds(k * (width // 2), width // 2)
        total = None
        for e in range(flight):
            term = dot(sel[e].astype(BF16), sums[e, :, cols], ((0,), (0,)))
            total = term if total is None else total + term
        gi_v[:, cols] = total.astype(BF16)
        write(gi_v.at[:, cols], gi_hbm.at[0, :, cols])
    for copy in copies:
        copy.wait()


def shards(inputs, upstream, route, prob, gate_up, down):
    sections = lax.axis_size("pipe")
    groups = lax.axis_size("expert")
    chips = groups // CORES
    flight = groups // SPLIT
    _, tokens, width = inputs.shape
    slots = route.shape[2]
    both_cols = gate_up.shape[3]
    hid = down.shape[2]
    dma = pltpu.SemaphoreType.DMA
    hbm = pl.BlockSpec(memory_space=pltpu.HBM)
    vmem = pl.BlockSpec(memory_space=pltpu.VMEM)
    kept = pltpu.VMEM
    ggu, gdn, sums, sel, x_t, grads = pl.pallas_call(
        functools.partial(exchange, sections, chips, flight),
        out_shape=(
            kept((width // 2, both_cols), BF16),
            kept((hid, width), BF16),
            kept((flight, CAP, width), BF16),
            kept((flight, CAP, tokens), F32),
            kept((width, groups * CAP), BF16),
            kept((groups * CAP, both_cols), BF16),
        ),
        in_specs=[hbm] * 6,
        out_specs=(vmem,) * 6,
        scratch_shapes=[
            pltpu.VMEM((tokens, width), BF16),
            pltpu.VMEM((tokens, width), BF16),
            pltpu.VMEM((slots, tokens), jnp.int32),
            pltpu.VMEM((slots, tokens), F32),
            pltpu.VMEM((width, both_cols), BF16),
            pltpu.VMEM((hid, width), BF16),
            pltpu.VMEM((flight, CAP, tokens), F32),
            pltpu.VMEM((flight, CAP, tokens), F32),
            pltpu.VMEM((flight, CAP, width), BF16),
            pltpu.VMEM((chips, CORES, CAP, width), BF16),
            pltpu.VMEM((flight, CAP, width), BF16),
            pltpu.VMEM((flight, CAP, width), BF16),
            pltpu.VMEM((chips, CORES, CAP, width), BF16),
            pltpu.VMEM((chips, CAP, width), BF16),
            pltpu.VMEM((chips, CORES, CAP, width), BF16),
            pltpu.VMEM((chips, CAP, width), BF16),
            pltpu.VMEM((chips, CAP, width), BF16),
            dma((6,)),
            dma((2,)),
            dma((chips,)),
            dma((chips,)),
            dma((chips,)),
            dma((chips,)),
            dma((E_PARTS,)),
            dma((E_PARTS,)),
            dma((E_PARTS, chips)),
            dma((E_PARTS, chips)),
            dma((E_PARTS, chips)),
            dma((E_PARTS, chips)),
            dma((OUT_PARTS,)),
            dma((OUT_PARTS,)),
            dma((OUT_PARTS, chips)),
            dma((OUT_PARTS, chips)),
        ],
        compiler_params=pltpu.CompilerParams(
            collective_id=0, has_side_effects=True, vmem_limit_bytes=40 * 2**20
        ),
    )(*(
        pltpu.with_memory_space_constraint(a, pltpu.HBM)
        for a in (inputs, upstream, jnp.swapaxes(route, 1, 2), jnp.swapaxes(prob, 1, 2), gate_up, down)
    ))
    return pl.pallas_call(
        functools.partial(finish, flight),
        out_shape=(
            jax.ShapeDtypeStruct(inputs.shape, BF16),
            jax.ShapeDtypeStruct(gate_up.shape, BF16),
            jax.ShapeDtypeStruct(down.shape, BF16),
        ),
        in_specs=[vmem] * 6,
        out_specs=(hbm,) * 3,
        scratch_shapes=[
            pltpu.VMEM((tokens, width), BF16),
            pltpu.VMEM((width // 2, both_cols), BF16),
            dma((4 + W_PARTS // 2,)),
        ],
        compiler_params=pltpu.CompilerParams(vmem_limit_bytes=16 * 2**20),
    )(ggu, gdn, sums, sel, x_t, grads)


def solution(mesh):
    placed = (
        P("pipe", "expert", None),
        P("pipe", "expert", None),
        P("pipe", "expert", None),
        P("pipe", "expert", None),
        P("pipe", "expert", None, None),
        P("pipe", "expert", None, None),
    )
    return jax.shard_map(
        shards,
        mesh=mesh,
        in_specs=placed,
        out_specs=(
            P("pipe", "expert", None),
            P("pipe", "expert", None, None),
            P("pipe", "expert", None, None),
        ),
        check_vma=False,
    )
```

```python
import functools

import jax
import jax.numpy as jnp
from jax import lax
from jax.experimental import pallas as pl
from jax.experimental.pallas import tpu as pltpu
from jax.sharding import PartitionSpec as P

SPLIT = 8
CAP = 8
CORES = 2
E_PARTS = 4
OUT_PARTS = 4
W_PARTS = 4
TURN_PARTS = 4
MESH = pl.DeviceIdType.MESH
F32 = jnp.float32
BF16 = jnp.bfloat16


def dot(a, b, dims):
    return lax.dot_general(a, b, (dims, ((), ())), preferred_element_type=F32)


def remote(src, dst, send, recv, target):
    return pltpu.make_async_remote_copy(
        src_ref=src, dst_ref=dst, send_sem=send, recv_sem=recv, device_id=target, device_id_type=MESH
    )


def exchange(
    sections, chips, flight,
    x_hbm, u_hbm, route_hbm, prob_hbm, gu_hbm, dn_hbm,
    ggu, gdn, sums, sel_out,
    x_v, u_v, route_v, prob_v, w_gu, w_dn, x_t,
    s_out, s_in, xb, xg, eb, er, eg, pair_in, keep, ro, rin,
    local, s_sem, x_send, x_recv, xf_send, xf_recv,
    z_send, z_recv, e_send, e_recv, ef_send, ef_recv,
    p_send, p_recv, r_send, r_recv,
):
    section = lax.axis_index("pipe")
    me = lax.axis_index("expert")
    chip, core = me // CORES, me % CORES
    mine = me // SPLIT
    sibling = {"expert": me + 1 - 2 * core}
    ahead = {"pipe": (section + 1) % sections}
    behind = {"pipe": (section + sections - 1) % sections}
    width = x_v.shape[1]
    tokens = x_v.shape[0]
    hid = w_dn.shape[0]

    def chip_at(d):
        at, bit = 0, 1
        while bit < chips:
            at = at + (chip // bit + d // bit) % 2 * bit
            bit *= 2
        return at

    def peer(d):
        return {"expert": chip_at(d) * CORES + core}

    loads = [
        pltpu.make_async_copy(src, dst, local.at[k])
        for k, (src, dst) in enumerate(
            (
                (route_hbm.at[0], route_v),
                (prob_hbm.at[0], prob_v),
                (x_hbm.at[0], x_v),
                (u_hbm.at[0], u_v),
                (gu_hbm.at[0, 0], w_gu),
                (dn_hbm.at[0, 0], w_dn),
            )
        )
    ]
    loads[0].start()
    loads[1].start()
    barrier = pltpu.get_barrier_semaphore()
    for target in [behind, sibling] + [peer(d) for d in range(1, chips)]:
        pl.semaphore_signal(barrier, inc=1, device_id=target, device_id_type=MESH)
    loads[2].start()
    loads[3].start()
    loads[0].wait()
    loads[1].wait()
    before = (
        lax.broadcasted_iota(jnp.int32, (tokens, tokens), 0)
        < lax.broadcasted_iota(jnp.int32, (tokens, tokens), 1)
    ).astype(F32).astype(BF16)
    slots = lax.broadcasted_iota(jnp.int32, (CAP, tokens), 0).astype(F32)
    picks = []
    for e in range(flight):
        hit = route_v[...] == e
        member = jnp.max(jnp.where(hit, 1.0, 0.0), axis=0, keepdims=True)
        weight = jnp.sum(jnp.where(hit, prob_v[...], 0.0), axis=0, keepdims=True)
        member = jnp.broadcast_to(member, (CAP, tokens))
        rank = dot(member.astype(BF16), before, ((1,), (0,)))
        chosen = jnp.where((member > 0.0) & (rank == slots), 1.0, 0.0)
        sel_out[e] = chosen
        s_out[e] = chosen * weight
        picks.append(chosen.astype(BF16))
    pl.semaphore_wait(barrier, chips + 1)

    send_s = remote(s_out, s_in, s_sem.at[0], s_sem.at[1], ahead)
    send_s.start()
    sends = [send_s]

    loads[2].wait()
    loads[5].start()
    loads[4].start()
    for e in range(flight):
        xb[e] = dot(picks[e], x_v[...], ((1,), (0,))).astype(BF16)
    for d in range(1, chips):
        copy = remote(
            xb.at[chip_at(d) * CORES // SPLIT], xg.at[d, core], x_send.at[d], x_recv.at[d], peer(d)
        )
        copy.start()
        sends.append(copy)
    copy = remote(xb.at[mine], xg.at[0, core], xf_send.at[0], xf_recv.at[0], sibling)
    copy.start()
    sends.append(copy)
    xg[0, core] = xb[mine]

    loads[3].wait()
    send_s.wait_recv()
    e_cols = width // E_PARTS
    scales, gpicks = [], []
    for e in range(flight):
        weights = s_in[e]
        scales.append(jnp.sum(weights, axis=1, keepdims=True))
        gpicks.append(jnp.where(weights > 0.0, 1.0, 0.0).astype(BF16))
    z_copies = []
    for k in range(E_PARTS):
        cols = pl.ds(k * e_cols, e_cols)
        for e in range(flight):
            eb[e, :, cols] = (dot(gpicks[e], u_v[:, cols], ((1,), (0,))) * scales[e]).astype(BF16)
        copy = remote(eb.at[:, :, cols], er.at[:, :, cols], z_send.at[k], z_recv.at[k], behind)
        copy.start()
        z_copies.append(copy)
    sends.extend(z_copies)

    def relay(buf, d, cols, recv, f_send, f_recv):
        slot = buf.at[d, core, :, cols]
        remote(slot, slot, f_send, recv, sibling).wait_recv()
        copy = remote(slot, slot, f_send, f_recv, sibling)
        copy.start()
        sends.append(copy)

    def from_sibling(buf, d, cols, f_send, f_recv):
        slot = buf.at[d, 1 - core, :, cols]
        remote(slot, slot, f_send, f_recv, sibling).wait_recv()

    def send_e(k, d):
        cols = pl.ds(k * e_cols, e_cols)
        copy = remote(
            er.at[chip_at(d) * CORES // SPLIT, :, cols],
            eg.at[d, core, :, cols],
            e_send.at[k, d],
            e_recv.at[k, d],
            peer(d),
        )
        copy.start()
        sends.append(copy)

    every = pl.ds(0, width)
    for k in range(E_PARTS):
        cols = pl.ds(k * e_cols, e_cols)
        z_copies[k].wait_recv()
        for d in range(1, chips):
            send_e(k, d)
        copy = remote(
            er.at[mine, :, cols], eg.at[0, core, :, cols], ef_send.at[k, 0], ef_recv.at[k, 0], sibling
        )
        copy.start()
        sends.append(copy)
        eg[0, core, :, cols] = er[mine, :, cols]
    for d in range(1, chips):
        relay(xg, d, every, x_recv.at[d], xf_send.at[d], xf_recv.at[d])
    loads[4].wait()
    loads[5].wait()
    for d in range(chips):
        from_sibling(xg, d, every, xf_send.at[d], xf_recv.at[d])
    rows = CORES * chips * CAP
    both = dot(xg[...].reshape(rows, width), w_gu[...], ((1,), (0,)))
    pre_gate = both[:, :hid]
    pre_up = both[:, hid:]
    sigma = jax.nn.sigmoid(pre_gate)
    silu_val = pre_gate * sigma
    hidden = (silu_val * pre_up).astype(BF16)
    slope = pre_up * sigma * (1.0 + pre_gate * (1.0 - sigma))

    o_cols = width // OUT_PARTS
    pair = {}
    t_cols = width // TURN_PARTS
    for k in range(TURN_PARTS):
        cols = pl.ds(k * t_cols, t_cols)
        x_t[cols, :] = xg[:, :, :, cols].reshape(rows, t_cols).T

    def to_pair(k):
        cols = pl.ds(k * o_cols, o_cols)
        part = dot(grad_both, w_gu[cols, :], ((1,), (1,))).astype(BF16)
        keep[:, :, :, cols] = part.reshape(chips, CORES, CAP, o_cols)
        copy = remote(
            keep.at[:, 1 - core, :, cols], pair_in.at[:, :, cols], p_send.at[k], p_recv.at[k], sibling
        )
        copy.start()
        pair[k] = copy
        sends.append(copy)

    def pass_on(k):
        cols = pl.ds(k * o_cols, o_cols)
        pair[k].wait_recv()
        ro[:, :, cols] = (keep[:, core, :, cols].astype(F32) + pair_in[:, :, cols].astype(F32)).astype(BF16)
        for d in range(1, chips):
            copy = remote(
                ro.at[d, :, cols], rin.at[chip, :, cols], r_send.at[k, d], r_recv.at[k, d], peer(d)
            )
            copy.start()
            sends.append(copy)
        rin[chip, :, cols] = ro[0, :, cols]

    grad_hidden = None
    for step in range(E_PARTS + 2):
        if step < E_PARTS:
            cols = pl.ds(step * e_cols, e_cols)
            for d in range(1, chips):
                relay(eg, d, cols, e_recv.at[step, d], ef_send.at[step, d], ef_recv.at[step, d])
        if step >= 2:
            k = step - 2
            cols = pl.ds(k * e_cols, e_cols)
            for d in range(chips):
                from_sibling(eg, d, cols, ef_send.at[k, d], ef_recv.at[k, d])
            term = dot(eg[:, :, :, cols].reshape(rows, e_cols), w_dn[:, cols], ((1,), (1,)))
            grad_hidden = term if grad_hidden is None else grad_hidden + term
    grad_both = jnp.concatenate([grad_hidden * slope, grad_hidden * silu_val], axis=1).astype(BF16)
    for k in range(OUT_PARTS):
        to_pair(k)
        if k > 0:
            pass_on(k - 1)
    w_cols = width // W_PARTS

    def weights_part(k):
        cols = pl.ds(k * w_cols, w_cols)
        e_part = eg[:, :, :, cols].reshape(rows, w_cols)
        gdn[:, cols] = dot(hidden, e_part, ((0,), (0,))).astype(BF16)
        ggu[cols, :] = dot(x_t[cols, :], grad_both, ((1,), (0,))).astype(BF16)

    weights_part(0)
    pass_on(OUT_PARTS - 1)
    for k in range(1, W_PARTS):
        weights_part(k)

    per = chips // flight
    for k in range(OUT_PARTS):
        cols = pl.ds(k * o_cols, o_cols)
        for d in range(1, chips):
            slot = rin.at[chip_at(d), :, cols]
            remote(slot, slot, r_send.at[k, d], r_recv.at[k, d], peer(d)).wait_recv()
        for e in range(flight):
            total = rin[e * per, :, cols].astype(F32)
            for q in range(1, per):
                total = total + rin[e * per + q, :, cols].astype(F32)
            sums[e, :, cols] = total.astype(BF16)
    for copy in sends:
        copy.wait_send()


def finish(flight, ggu, gdn, sums, sel, gi_hbm, gu_hbm, dn_hbm, gi_v, sems):
    copies = [
        pltpu.make_async_copy(ggu, gu_hbm.at[0, 0], sems.at[0]),
        pltpu.make_async_copy(gdn, dn_hbm.at[0, 0], sems.at[1]),
    ]
    for copy in copies:
        copy.start()
    total = None
    for e in range(flight):
        term = dot(sel[e].astype(BF16), sums[e], ((0,), (0,)))
        total = term if total is None else total + term
    gi_v[...] = total.astype(BF16)
    last = pltpu.make_async_copy(gi_v, gi_hbm.at[0], sems.at[2])
    last.start()
    for copy in copies + [last]:
        copy.wait()


def shards(inputs, upstream, route, prob, gate_up, down):
    sections = lax.axis_size("pipe")
    groups = lax.axis_size("expert")
    chips = groups // CORES
    flight = groups // SPLIT
    _, tokens, width = inputs.shape
    slots = route.shape[2]
    both_cols = gate_up.shape[3]
    hid = down.shape[2]
    dma = pltpu.SemaphoreType.DMA
    hbm = pl.BlockSpec(memory_space=pltpu.HBM)
    vmem = pl.BlockSpec(memory_space=pltpu.VMEM)
    kept = pltpu.VMEM
    ggu, gdn, sums, sel = pl.pallas_call(
        functools.partial(exchange, sections, chips, flight),
        out_shape=(
            kept((width, both_cols), BF16),
            kept((hid, width), BF16),
            kept((flight, CAP, width), BF16),
            kept((flight, CAP, tokens), F32),
        ),
        in_specs=[hbm] * 6,
        out_specs=(vmem,) * 4,
        scratch_shapes=[
            pltpu.VMEM((tokens, width), BF16),
            pltpu.VMEM((tokens, width), BF16),
            pltpu.VMEM((slots, tokens), jnp.int32),
            pltpu.VMEM((slots, tokens), F32),
            pltpu.VMEM((width, both_cols), BF16),
            pltpu.VMEM((hid, width), BF16),
            pltpu.VMEM((width, groups * CAP), BF16),
            pltpu.VMEM((flight, CAP, tokens), F32),
            pltpu.VMEM((flight, CAP, tokens), F32),
            pltpu.VMEM((flight, CAP, width), BF16),
            pltpu.VMEM((chips, CORES, CAP, width), BF16),
            pltpu.VMEM((flight, CAP, width), BF16),
            pltpu.VMEM((flight, CAP, width), BF16),
            pltpu.VMEM((chips, CORES, CAP, width), BF16),
            pltpu.VMEM((chips, CAP, width), BF16),
            pltpu.VMEM((chips, CORES, CAP, width), BF16),
            pltpu.VMEM((chips, CAP, width), BF16),
            pltpu.VMEM((chips, CAP, width), BF16),
            dma((6,)),
            dma((2,)),
            dma((chips,)),
            dma((chips,)),
            dma((chips,)),
            dma((chips,)),
            dma((E_PARTS,)),
            dma((E_PARTS,)),
            dma((E_PARTS, chips)),
            dma((E_PARTS, chips)),
            dma((E_PARTS, chips)),
            dma((E_PARTS, chips)),
            dma((OUT_PARTS,)),
            dma((OUT_PARTS,)),
            dma((OUT_PARTS, chips)),
            dma((OUT_PARTS, chips)),
        ],
        compiler_params=pltpu.CompilerParams(
            collective_id=0, has_side_effects=True, vmem_limit_bytes=40 * 2**20
        ),
    )(*(
        pltpu.with_memory_space_constraint(a, pltpu.HBM)
        for a in (inputs, upstream, jnp.swapaxes(route, 1, 2), jnp.swapaxes(prob, 1, 2), gate_up, down)
    ))
    return pl.pallas_call(
        functools.partial(finish, flight),
        out_shape=(
            jax.ShapeDtypeStruct(inputs.shape, BF16),
            jax.ShapeDtypeStruct(gate_up.shape, BF16),
            jax.ShapeDtypeStruct(down.shape, BF16),
        ),
        in_specs=[vmem] * 4,
        out_specs=(hbm,) * 3,
        scratch_shapes=[pltpu.VMEM((tokens, width), BF16), dma((3,))],
        compiler_params=pltpu.CompilerParams(vmem_limit_bytes=16 * 2**20),
    )(ggu, gdn, sums, sel)


def solution(mesh):
    placed = (
        P("pipe", "expert", None),
        P("pipe", "expert", None),
        P("pipe", "expert", None),
        P("pipe", "expert", None),
        P("pipe", "expert", None, None),
        P("pipe", "expert", None, None),
    )
    return jax.shard_map(
        shards,
        mesh=mesh,
        in_specs=placed,
        out_specs=(
            P("pipe", "expert", None),
            P("pipe", "expert", None, None),
            P("pipe", "expert", None, None),
        ),
        check_vma=False,
    )
```

```python
import functools

import jax
import jax.numpy as jnp
from jax import lax
from jax.experimental import pallas as pl
from jax.experimental.pallas import tpu as pltpu
from jax.sharding import PartitionSpec as P

SPLIT = 8
CAP = 8
CORES = 2
E_PARTS = 4
OUT_PARTS = 4
W_PARTS = 4
TURN_PARTS = 4
MESH = pl.DeviceIdType.MESH
F32 = jnp.float32
BF16 = jnp.bfloat16


def dot(a, b, dims):
    return lax.dot_general(a, b, (dims, ((), ())), preferred_element_type=F32)


def remote(src, dst, send, recv, target):
    return pltpu.make_async_remote_copy(
        src_ref=src, dst_ref=dst, send_sem=send, recv_sem=recv, device_id=target, device_id_type=MESH
    )


def exchange(
    sections, chips, flight,
    x_hbm, u_hbm, route_hbm, prob_hbm, gu_hbm, dn_hbm,
    ggu, gdn, sums, sel_out,
    x_v, u_v, route_v, prob_v, w_gu, w_dn, x_t,
    s_out, s_in, xb, xg, eb, er, eg, pair_in, keep, ro, rin,
    local, s_sem, x_send, x_recv, xf_send, xf_recv,
    z_send, z_recv, e_send, e_recv, ef_send, ef_recv,
    p_send, p_recv, r_send, r_recv,
):
    section = lax.axis_index("pipe")
    me = lax.axis_index("expert")
    chip, core = me // CORES, me % CORES
    mine = me // SPLIT
    sibling = {"expert": me + 1 - 2 * core}
    ahead = {"pipe": (section + 1) % sections}
    behind = {"pipe": (section + sections - 1) % sections}
    width = x_v.shape[1]
    tokens = x_v.shape[0]
    hid = w_dn.shape[0]

    def chip_at(d):
        at, bit = 0, 1
        while bit < chips:
            at = at + (chip // bit + d // bit) % 2 * bit
            bit *= 2
        return at

    def peer(d):
        return {"expert": chip_at(d) * CORES + core}

    loads = [
        pltpu.make_async_copy(src, dst, local.at[k])
        for k, (src, dst) in enumerate(
            (
                (route_hbm.at[0], route_v),
                (prob_hbm.at[0], prob_v),
                (x_hbm.at[0], x_v),
                (u_hbm.at[0], u_v),
                (gu_hbm.at[0, 0], w_gu),
                (dn_hbm.at[0, 0], w_dn),
            )
        )
    ]
    loads[0].start()
    loads[1].start()
    barrier = pltpu.get_barrier_semaphore()
    for target in [behind, sibling] + [peer(d) for d in range(1, chips)]:
        pl.semaphore_signal(barrier, inc=1, device_id=target, device_id_type=MESH)
    loads[2].start()
    loads[3].start()
    loads[0].wait()
    loads[1].wait()
    before = (
        lax.broadcasted_iota(jnp.int32, (tokens, tokens), 0)
        < lax.broadcasted_iota(jnp.int32, (tokens, tokens), 1)
    ).astype(F32).astype(BF16)
    slots = lax.broadcasted_iota(jnp.int32, (CAP, tokens), 0).astype(F32)
    picks = []
    for e in range(flight):
        hit = route_v[...] == e
        member = jnp.max(jnp.where(hit, 1.0, 0.0), axis=0, keepdims=True)
        weight = jnp.sum(jnp.where(hit, prob_v[...], 0.0), axis=0, keepdims=True)
        member = jnp.broadcast_to(member, (CAP, tokens))
        rank = dot(member.astype(BF16), before, ((1,), (0,)))
        chosen = jnp.where((member > 0.0) & (rank == slots), 1.0, 0.0)
        sel_out[e] = chosen
        s_out[e] = chosen * weight
        picks.append(chosen.astype(BF16))
    pl.semaphore_wait(barrier, chips + 1)

    send_s = remote(s_out, s_in, s_sem.at[0], s_sem.at[1], ahead)
    send_s.start()
    sends = [send_s]

    loads[2].wait()
    loads[5].start()
    loads[4].start()
    for e in range(flight):
        xb[e] = dot(picks[e], x_v[...], ((1,), (0,))).astype(BF16)
    for d in range(1, chips):
        copy = remote(
            xb.at[chip_at(d) * CORES // SPLIT], xg.at[d, core], x_send.at[d], x_recv.at[d], peer(d)
        )
        copy.start()
        sends.append(copy)
    copy = remote(xb.at[mine], xg.at[0, core], xf_send.at[0], xf_recv.at[0], sibling)
    copy.start()
    sends.append(copy)
    xg[0, core] = xb[mine]

    loads[3].wait()
    send_s.wait_recv()
    e_cols = width // E_PARTS
    scales, gpicks = [], []
    for e in range(flight):
        weights = s_in[e]
        scales.append(jnp.sum(weights, axis=1, keepdims=True))
        gpicks.append(jnp.where(weights > 0.0, 1.0, 0.0).astype(BF16))
    z_copies = []
    for k in range(E_PARTS):
        cols = pl.ds(k * e_cols, e_cols)
        for e in range(flight):
            eb[e, :, cols] = (dot(gpicks[e], u_v[:, cols], ((1,), (0,))) * scales[e]).astype(BF16)
        copy = remote(eb.at[:, :, cols], er.at[:, :, cols], z_send.at[k], z_recv.at[k], behind)
        copy.start()
        z_copies.append(copy)
    sends.extend(z_copies)

    def relay(buf, d, cols, recv, f_send, f_recv):
        slot = buf.at[d, core, :, cols]
        remote(slot, slot, f_send, recv, sibling).wait_recv()
        copy = remote(slot, slot, f_send, f_recv, sibling)
        copy.start()
        sends.append(copy)

    def from_sibling(buf, d, cols, f_send, f_recv):
        slot = buf.at[d, 1 - core, :, cols]
        remote(slot, slot, f_send, f_recv, sibling).wait_recv()

    def send_e(k, d):
        cols = pl.ds(k * e_cols, e_cols)
        copy = remote(
            er.at[chip_at(d) * CORES // SPLIT, :, cols],
            eg.at[d, core, :, cols],
            e_send.at[k, d],
            e_recv.at[k, d],
            peer(d),
        )
        copy.start()
        sends.append(copy)

    every = pl.ds(0, width)
    for k in range(E_PARTS):
        cols = pl.ds(k * e_cols, e_cols)
        z_copies[k].wait_recv()
        for d in range(1, chips):
            send_e(k, d)
        copy = remote(
            er.at[mine, :, cols], eg.at[0, core, :, cols], ef_send.at[k, 0], ef_recv.at[k, 0], sibling
        )
        copy.start()
        sends.append(copy)
        eg[0, core, :, cols] = er[mine, :, cols]
    for d in range(1, chips):
        relay(xg, d, every, x_recv.at[d], xf_send.at[d], xf_recv.at[d])
    loads[4].wait()
    loads[5].wait()
    for d in range(chips):
        from_sibling(xg, d, every, xf_send.at[d], xf_recv.at[d])
    rows = CORES * chips * CAP
    both = dot(xg[...].reshape(rows, width), w_gu[...], ((1,), (0,)))
    pre_gate = both[:, :hid]
    pre_up = both[:, hid:]
    sigma = jax.nn.sigmoid(pre_gate)
    silu_val = pre_gate * sigma
    hidden = (silu_val * pre_up).astype(BF16)
    slope = pre_up * sigma * (1.0 + pre_gate * (1.0 - sigma))

    o_cols = width // OUT_PARTS
    pair = {}
    t_cols = width // TURN_PARTS
    for k in range(TURN_PARTS):
        cols = pl.ds(k * t_cols, t_cols)
        x_t[cols, :] = xg[:, :, :, cols].reshape(rows, t_cols).T

    def to_pair(k):
        cols = pl.ds(k * o_cols, o_cols)
        part = dot(grad_both, w_gu[cols, :], ((1,), (1,))).astype(BF16)
        keep[:, :, :, cols] = part.reshape(chips, CORES, CAP, o_cols)
        copy = remote(
            keep.at[:, 1 - core, :, cols], pair_in.at[:, :, cols], p_send.at[k], p_recv.at[k], sibling
        )
        copy.start()
        pair[k] = copy
        sends.append(copy)

    def pass_on(k):
        cols = pl.ds(k * o_cols, o_cols)
        pair[k].wait_recv()
        ro[:, :, cols] = (keep[:, core, :, cols].astype(F32) + pair_in[:, :, cols].astype(F32)).astype(BF16)
        for d in range(1, chips):
            copy = remote(
                ro.at[d, :, cols], rin.at[chip, :, cols], r_send.at[k, d], r_recv.at[k, d], peer(d)
            )
            copy.start()
            sends.append(copy)
        rin[chip, :, cols] = ro[0, :, cols]

    grad_hidden = None
    for step in range(E_PARTS + 2):
        if step < E_PARTS:
            cols = pl.ds(step * e_cols, e_cols)
            for d in range(1, chips):
                relay(eg, d, cols, e_recv.at[step, d], ef_send.at[step, d], ef_recv.at[step, d])
        if step >= 2:
            k = step - 2
            cols = pl.ds(k * e_cols, e_cols)
            for d in range(chips):
                from_sibling(eg, d, cols, ef_send.at[k, d], ef_recv.at[k, d])
            term = dot(eg[:, :, :, cols].reshape(rows, e_cols), w_dn[:, cols], ((1,), (1,)))
            grad_hidden = term if grad_hidden is None else grad_hidden + term
    grad_both = jnp.concatenate([grad_hidden * slope, grad_hidden * silu_val], axis=1).astype(BF16)
    for k in range(OUT_PARTS):
        to_pair(k)
        if k > 0:
            pass_on(k - 1)
    w_cols = width // W_PARTS

    def weights_part(k):
        cols = pl.ds(k * w_cols, w_cols)
        e_part = eg[:, :, :, cols].reshape(rows, w_cols)
        gdn[:, cols] = dot(hidden, e_part, ((0,), (0,))).astype(BF16)
        ggu[cols, :] = dot(x_t[cols, :], grad_both, ((1,), (0,))).astype(BF16)

    pass_on(OUT_PARTS - 1)
    for k in range(W_PARTS):
        weights_part(k)

    per = chips // flight
    for k in range(OUT_PARTS):
        cols = pl.ds(k * o_cols, o_cols)
        for d in range(1, chips):
            slot = rin.at[chip_at(d), :, cols]
            remote(slot, slot, r_send.at[k, d], r_recv.at[k, d], peer(d)).wait_recv()
        for e in range(flight):
            total = rin[e * per, :, cols].astype(F32)
            for q in range(1, per):
                total = total + rin[e * per + q, :, cols].astype(F32)
            sums[e, :, cols] = total.astype(BF16)
    for copy in sends:
        copy.wait_send()


def finish(flight, ggu, gdn, sums, sel, gi_hbm, gu_hbm, dn_hbm, gi_v, sems):
    copies = [
        pltpu.make_async_copy(ggu, gu_hbm.at[0, 0], sems.at[0]),
        pltpu.make_async_copy(gdn, dn_hbm.at[0, 0], sems.at[1]),
    ]
    for copy in copies:
        copy.start()
    total = None
    for e in range(flight):
        term = dot(sel[e].astype(BF16), sums[e], ((0,), (0,)))
        total = term if total is None else total + term
    gi_v[...] = total.astype(BF16)
    last = pltpu.make_async_copy(gi_v, gi_hbm.at[0], sems.at[2])
    last.start()
    for copy in copies + [last]:
        copy.wait()


def shards(inputs, upstream, route, prob, gate_up, down):
    sections = lax.axis_size("pipe")
    groups = lax.axis_size("expert")
    chips = groups // CORES
    flight = groups // SPLIT
    _, tokens, width = inputs.shape
    slots = route.shape[2]
    both_cols = gate_up.shape[3]
    hid = down.shape[2]
    dma = pltpu.SemaphoreType.DMA
    hbm = pl.BlockSpec(memory_space=pltpu.HBM)
    vmem = pl.BlockSpec(memory_space=pltpu.VMEM)
    kept = pltpu.VMEM
    ggu, gdn, sums, sel = pl.pallas_call(
        functools.partial(exchange, sections, chips, flight),
        out_shape=(
            kept((width, both_cols), BF16),
            kept((hid, width), BF16),
            kept((flight, CAP, width), BF16),
            kept((flight, CAP, tokens), F32),
        ),
        in_specs=[hbm] * 6,
        out_specs=(vmem,) * 4,
        scratch_shapes=[
            pltpu.VMEM((tokens, width), BF16),
            pltpu.VMEM((tokens, width), BF16),
            pltpu.VMEM((slots, tokens), jnp.int32),
            pltpu.VMEM((slots, tokens), F32),
            pltpu.VMEM((width, both_cols), BF16),
            pltpu.VMEM((hid, width), BF16),
            pltpu.VMEM((width, groups * CAP), BF16),
            pltpu.VMEM((flight, CAP, tokens), F32),
            pltpu.VMEM((flight, CAP, tokens), F32),
            pltpu.VMEM((flight, CAP, width), BF16),
            pltpu.VMEM((chips, CORES, CAP, width), BF16),
            pltpu.VMEM((flight, CAP, width), BF16),
            pltpu.VMEM((flight, CAP, width), BF16),
            pltpu.VMEM((chips, CORES, CAP, width), BF16),
            pltpu.VMEM((chips, CAP, width), BF16),
            pltpu.VMEM((chips, CORES, CAP, width), BF16),
            pltpu.VMEM((chips, CAP, width), BF16),
            pltpu.VMEM((chips, CAP, width), BF16),
            dma((6,)),
            dma((2,)),
            dma((chips,)),
            dma((chips,)),
            dma((chips,)),
            dma((chips,)),
            dma((E_PARTS,)),
            dma((E_PARTS,)),
            dma((E_PARTS, chips)),
            dma((E_PARTS, chips)),
            dma((E_PARTS, chips)),
            dma((E_PARTS, chips)),
            dma((OUT_PARTS,)),
            dma((OUT_PARTS,)),
            dma((OUT_PARTS, chips)),
            dma((OUT_PARTS, chips)),
        ],
        compiler_params=pltpu.CompilerParams(
            collective_id=0, has_side_effects=True, vmem_limit_bytes=40 * 2**20
        ),
    )(*(
        pltpu.with_memory_space_constraint(a, pltpu.HBM)
        for a in (inputs, upstream, jnp.swapaxes(route, 1, 2), jnp.swapaxes(prob, 1, 2), gate_up, down)
    ))
    return pl.pallas_call(
        functools.partial(finish, flight),
        out_shape=(
            jax.ShapeDtypeStruct(inputs.shape, BF16),
            jax.ShapeDtypeStruct(gate_up.shape, BF16),
            jax.ShapeDtypeStruct(down.shape, BF16),
        ),
        in_specs=[vmem] * 4,
        out_specs=(hbm,) * 3,
        scratch_shapes=[pltpu.VMEM((tokens, width), BF16), dma((3,))],
        compiler_params=pltpu.CompilerParams(vmem_limit_bytes=16 * 2**20),
    )(ggu, gdn, sums, sel)


def solution(mesh):
    placed = (
        P("pipe", "expert", None),
        P("pipe", "expert", None),
        P("pipe", "expert", None),
        P("pipe", "expert", None),
        P("pipe", "expert", None, None),
        P("pipe", "expert", None, None),
    )
    return jax.shard_map(
        shards,
        mesh=mesh,
        in_specs=placed,
        out_specs=(
            P("pipe", "expert", None),
            P("pipe", "expert", None, None),
            P("pipe", "expert", None, None),
        ),
        check_vma=False,
    )
```
